32 devices in a mesh: groups: 2 (over x), pts: 16 (over z, y, core).
Axes of the slice: x: 2, y: 2, z: 4, core: 2. Of those that a mesh axis runs over, the one named last changes fastest.
Arguments:
- points: bfloat16 [8192, 512], P(('groups', 'pts')), parts along dimension 0, may hold values from -6 to 6
- labels: int32 [8192], P(('groups', 'pts')), parts along dimension 0, may hold values from 0 to 15
- centres: bfloat16 [32768, 512], P(('groups', 'pts')), parts along dimension 0, may hold values from -6 to 6
- tri_inverse: bfloat16 [32768, 16384], P(('groups', 'pts')), parts along dimension 0, as said below
- beta: bfloat16 [32768, 16], P(('groups', 'pts')), parts along dimension 0, may hold values from -0.01171875 to 0.01171875
- bias: float32 [32], P('groups'), parts along dimension 0, may hold values from -3.2 to -2.2
Outputs:
- gradient: float32 [32768, 16], P(('groups', 'pts')), parts along dimension 0
- logits: float32 [8192, 16], P(('groups', 'pts')), parts along dimension 0
The draws below stay inside these ranges and needn't reach their ends.
There are 2 independent parts, one for each index of `groups`. The reference program is written for one: setup_inputs(seed, part) draws one part's arguments, and reference() takes and returns one part's arrays. A program takes and returns all parts, laid end to end along the dimension named above; each array names one. Nothing has to cross between parts.
Inputs may be any that keep to these rules, and one draw needn't show every extreme that they name: `tri_inverse`: upper triangular: entries below the diagonal are zero; the diagonal lies between 0.6 and 1.4.
All inputs are finite; a program needn't handle non-finite values.
Results may differ from the reference program's by a relative error of at most 0.0039.
Values may be sent and summed in bfloat16 or wider, within the bound.
No kernel may reach another device: no remote copies, remote signals or barrier semaphores. Data moves between devices by JAX's collectives and lax.ppermute only.
A program may use at most 128 MiB of HBM per device.

```python
import math
import jax
import jax.numpy as jnp
from jax import lax

CENTRES = 16384
FEATURES = 512
CLASSES = 16
POINTS = 4096


def draw_tri_inverse(key, part):
    key_off, key_diag = jax.random.split(jax.random.fold_in(key, 7))
    offdiag = jax.random.normal(key_off, (CENTRES, CENTRES), jnp.float32) * (0.5 * CENTRES ** (-0.5))
    diagonal = jax.random.uniform(key_diag, (CENTRES,), jnp.float32, 0.6, 1.4)
    row_index = jnp.arange(CENTRES)[:, None]
    col_index = jnp.arange(CENTRES)[None, :]
    result = jnp.where(col_index > row_index, offdiag, 0.0)
    result = jnp.where(col_index == row_index, diagonal[:, None], result)
    return result.astype(jnp.bfloat16)


def place_ends(drawn, stream_key, least, high):
    spot = [jax.random.randint(jax.random.fold_in(stream_key, axis), (), 0, length) for axis, length in enumerate(drawn.shape)]
    main_axis = drawn.shape.index(max(drawn.shape))
    beside = spot[:main_axis] + [(spot[main_axis] + 1) % drawn.shape[main_axis]] + spot[main_axis + 1:]
    return drawn.at[tuple(spot)].set(least).at[tuple(beside)].set(high)


def steps_of(key, shape, shards, low, largest):
    loudness = 1.0
    for axis_at, blocks in shards:
        draws = jax.random.uniform(jax.random.fold_in(jax.random.fold_in(key, 6), axis_at), (blocks,), jnp.float32, low / len(shards), largest / len(shards))
        loudness = loudness * jnp.repeat(jnp.exp(draws), shape[axis_at] // blocks).reshape((-1,) + (1,) * (len(shape) - 1 - axis_at))
    return loudness


def scatter_about(rng, dims, spread, bound, cuts=(), held_as=jnp.bfloat16):
    values = spread * jax.random.normal(rng, dims, jnp.float32)
    if cuts:
        values = values * steps_of(rng, dims, cuts, -0.22, 0.18)
    return jnp.clip(values, -bound, bound).astype(held_as)


def setup_inputs(seed: int = 0, part: int = 0) -> dict:
    key_list = jax.random.split(jax.random.key(seed), 7)
    part_splits = jax.random.split(jax.random.fold_in(key_list[6], part), 7)
    return {
        "points": scatter_about(part_splits[0], (POINTS, FEATURES), 1.0, 6.0, ((0, 16),)),
        "labels": place_ends(jax.random.randint(part_splits[1], (POINTS,), 0, CLASSES), jax.random.fold_in(part_splits[1], 1), 0, CLASSES - 1).astype(jnp.int32),
        "centres": scatter_about(part_splits[2], (CENTRES, FEATURES), 1.0, 6.0, ((0, 16),)),
        "tri_inverse": draw_tri_inverse(jax.random.fold_in(jax.random.fold_in(key_list[6], part), 71), part),
        "beta": scatter_about(part_splits[4], (CENTRES, CLASSES), (16 * CENTRES) ** -0.5, 0.01171875, ((0, 16),)),
        "bias": jnp.clip(jax.random.uniform(part_splits[5], (CLASSES,), jnp.float32, -3.2, -2.2), -3.2, -2.2),
    }


def cube_kernel(point_block, centre_all):
    inner = jnp.dot(point_block, centre_all.T, preferred_element_type=jnp.float32)
    factor = 1.0 / math.sqrt(FEATURES)
    return ((inner * factor + 1.0) ** 3).astype(jnp.bfloat16)

def reference(points, labels, centres, tri_inverse, beta, bias):
    alpha = jnp.dot(tri_inverse, beta, preferred_element_type=jnp.float32).astype(jnp.bfloat16)
    block_size = math.gcd(POINTS, 1024)
    block_count = POINTS // block_size
    point_blocks = points.reshape(block_count, block_size, FEATURES)
    label_blocks = labels.reshape(block_count, block_size)
    classes_row = jnp.arange(CLASSES, dtype=jnp.int32)

    def advance(running, inputs):
        point_block, label_block = inputs
        kernel_tile = cube_kernel(point_block, centres)
        block_logits = jnp.dot(kernel_tile, alpha, preferred_element_type=jnp.float32) + bias[None, :]
        onehot = (label_block[:, None] == classes_row[None, :]).astype(jnp.float32)
        resid = (jax.nn.sigmoid(block_logits) - onehot).astype(jnp.bfloat16)
        update = lax.dot_general(kernel_tile, resid, (((0,), (0,)), ((), ())), preferred_element_type=jnp.float32)
        return (running + update, block_logits)
    grad_sum, logit_blocks = lax.scan(advance, jnp.zeros((CENTRES, CLASSES), jnp.float32), (point_blocks, label_blocks))
    grad_kernel = (grad_sum * (1.0 / math.sqrt(POINTS))).astype(jnp.bfloat16)
    gradient = lax.dot_general(tri_inverse, grad_kernel, (((0,), (0,)), ((), ())), preferred_element_type=jnp.float32)
    return (gradient, logit_blocks.reshape(POINTS, CLASSES))
```

```python
import math

import jax
import jax.numpy as jnp
from jax import lax
from jax.experimental import pallas as pl
from jax.experimental.pallas import tpu as pltpu
from jax.sharding import PartitionSpec as P

BF16 = jnp.bfloat16
F32 = jnp.float32
ROWS_BY_ROWS = (((1,), (1,)), ((), ()))
MIB = 1 << 20
IN_FLIGHT = 3


def params(mib):
    return pltpu.CompilerParams(vmem_limit_bytes=mib * MIB)


def in_vmem():
    return pl.BlockSpec(memory_space=pltpu.VMEM)


def anywhere():
    return pl.BlockSpec(memory_space=pl.ANY)


def in_smem():
    return pl.BlockSpec(memory_space=pltpu.SMEM)


def cost(flops, bytes_accessed):
    return pl.CostEstimate(flops=int(flops), bytes_accessed=int(bytes_accessed), transcendentals=0)


def alpha_step(me, offsets, coeffs, tri, total, last):
    rows = tri.shape[0]
    count, classes, width = coeffs.shape
    ahead = min(IN_FLIGHT, count)

    def body(*refs):
        me_ref, tri_ref, coeff_ref = refs[:3]
        out_ref, held_ref, sems = refs[-3:]
        copies = [
            pltpu.make_async_copy(
                tri_ref.at[:, pl.ds(pl.multiple_of((me_ref[0] ^ offset) * width, width), width)],
                held_ref.at[at],
                sems.at[at],
            )
            for at, offset in enumerate(offsets)
        ]
        for copy in copies[:ahead]:
            copy.start()
        acc = None if total is None else refs[3][...]
        for at in range(count):
            copies[at].wait()
            if at + ahead < count:
                copies[at + ahead].start()
            term = lax.dot_general(coeff_ref[at], held_ref[at], ROWS_BY_ROWS, preferred_element_type=F32)
            acc = term if acc is None else acc + term
        out_ref[...] = acc.astype(out_ref.dtype)

    operands = (me, tri, coeffs) + (() if total is None else (total,))
    return pl.pallas_call(
        body,
        out_shape=[
            jax.ShapeDtypeStruct((classes, rows), BF16 if last else F32),
            pltpu.VMEM((count, rows, width), BF16),
        ],
        in_specs=[in_smem(), anywhere()] + [in_vmem()] * (len(operands) - 2),
        out_specs=[in_vmem(), in_vmem()],
        scratch_shapes=[pltpu.SemaphoreType.DMA((count,))],
        compiler_params=params(8),
        cost_estimate=cost(2 * rows * count * width * 128, 2 * rows * count * width),
        name="alpha_step",
    )(*operands)


def gradient_terms(grad, blocks, first, count):
    classes, rows = grad.shape
    width = blocks.shape[2]

    def body(grad_ref, block_ref, out_ref):
        for at in range(count):
            out_ref[at] = jnp.dot(grad_ref[...], block_ref[first + at], preferred_element_type=F32)

    return pl.pallas_call(
        body,
        out_shape=jax.ShapeDtypeStruct((count, classes, width), F32),
        in_specs=[in_vmem(), in_vmem()],
        out_specs=in_vmem(),
        compiler_params=params(8),
        cost_estimate=cost(2 * rows * count * width * 128, 1024),
        name="gradient_terms",
    )(grad, pltpu.with_memory_space_constraint(blocks, pltpu.VMEM))


def kernel_tile(points, centre_blocks, after):
    block, features = points[0].shape
    local = sum(piece.shape[0] for piece in centre_blocks[0])
    factor = 1.0 / math.sqrt(features)
    pieces = [piece for pieces in centre_blocks for piece in pieces]
    total = len(points) * block

    def body(*refs):
        point_refs, piece_refs, out_ref = refs[: len(points)], refs[len(points) : -2], refs[-1]
        row = 0
        for piece_ref in piece_refs:
            which, first, rows = row // local, row % local, piece_ref.shape[0]
            for at, point_ref in enumerate(point_refs):
                inner = lax.dot_general(
                    piece_ref[...], point_ref[...], ROWS_BY_ROWS, preferred_element_type=F32
                )
                value = inner * factor + 1.0
                out_ref[which, first : first + rows, at * block : (at + 1) * block] = (
                    value * value * value
                ).astype(BF16)
            row += rows

    return pl.pallas_call(
        body,
        out_shape=pltpu.VMEM((len(centre_blocks), local, total), BF16),
        in_specs=[in_vmem()] * (len(points) + len(pieces)) + [anywhere()],
        out_specs=in_vmem(),
        compiler_params=params(8),
        cost_estimate=cost(2 * total * len(centre_blocks) * local * features, 1024),
        name="kernel_tile",
    )(*points, *pieces, after)


def partial_logits(tiles, alphas):
    classes = alphas[0].shape[0]
    sizes = [row[0].shape[2] for row in tiles]
    flat = [tile for row in tiles for tile in row]
    counts = [tile.shape[0] for tile in tiles[0]]

    def body(*refs):
        alpha_refs, tile_refs, out_ref = refs[: len(alphas)], refs[len(alphas) : -1], refs[-1]
        for part, size in enumerate(sizes):
            first = sum(sizes[:part])
            acc = None
            index = 0
            for which, count in enumerate(counts):
                tile_ref = tile_refs[part * len(counts) + which]
                for at in range(count):
                    term = jnp.dot(alpha_refs[index][...], tile_ref[at], preferred_element_type=F32)
                    acc = term if acc is None else acc + term
                    index += 1
            out_ref[:, first : first + size] = acc

    return pl.pallas_call(
        body,
        out_shape=jax.ShapeDtypeStruct((classes, sum(sizes)), F32),
        in_specs=[in_vmem()] * (len(alphas) + len(flat)),
        out_specs=in_vmem(),
        compiler_params=params(8),
        cost_estimate=cost(2 * sum(tile.size for tile in flat) * 128, 1024),
        name="partial_logits",
    )(*alphas, *flat)


def kernel_gradient(logit_sum, received, order, bias, onehots, hot_order, tiles):
    flat = [tile for row in tiles for tile in row]
    n_parts = len(tiles[0])
    local = flat[0].shape[1]
    sizes = [row[0].shape[2] for row in tiles]
    classes, total = logit_sum.shape
    block = total // len(order)

    def body(sum_ref, received_ref, bias_ref, onehot_ref, *refs):
        tile_refs, out_refs, (logits_ref, resid_ref) = refs[: len(flat)], refs[len(flat) : -2], refs[-2:]
        for at, source in enumerate(order):
            here = slice(at * block, (at + 1) * block)
            there = slice(source * block, (source + 1) * block)
            logits = sum_ref[:, here] + received_ref[:, there] + bias_ref[:, :1]
            if at == 0:
                logits_ref[...] = logits
            resid_ref[:, here] = (jax.nn.sigmoid(logits) - onehot_ref[hot_order[at]].astype(F32)).astype(BF16)
        for parity, out_ref in enumerate(out_refs):
            for which in range(n_parts):
                acc = None
                for part, size in enumerate(sizes):
                    first = sum(sizes[:part])
                    term = lax.dot_general(
                        resid_ref[:, first : first + size],
                        tile_refs[part * n_parts + which][parity],
                        ROWS_BY_ROWS,
                        preferred_element_type=F32,
                    )
                    acc = term if acc is None else acc + term
                out_ref[which] = acc

    return pl.pallas_call(
        body,
        out_shape=[jax.ShapeDtypeStruct((n_parts, classes, local), F32)] * 2
        + [jax.ShapeDtypeStruct((classes, block), F32)],
        in_specs=[in_vmem()] * (4 + len(flat)),
        out_specs=[in_vmem()] * 3,
        scratch_shapes=[pltpu.VMEM((classes, total), BF16)],
        compiler_params=params(8),
        cost_estimate=cost(2 * sum(tile.size for tile in flat) * 128, 1024),
        name="kernel_gradient",
    )(logit_sum, received, bias, onehots, *flat)


def on_device(points, labels, centres, tri_inverse, beta, bias):
    devices = lax.axis_size("pts")
    local_centres, classes = beta.shape
    total_points = points.shape[0] * devices
    outer = [1 << bit for bit in range(2, devices.bit_length() - 1)]

    def swap(array, mask):
        return lax.ppermute(array, "pts", [(index, index ^ mask) for index in range(devices)])

    tri_inverse = pltpu.with_memory_space_constraint(tri_inverse, pltpu.HBM)
    me = lax.axis_index("pts").astype(jnp.int32).reshape(1)
    bias_column = jnp.broadcast_to(bias[:, None], (classes, 128))
    class_column = jnp.arange(classes, dtype=jnp.int32)[:, None]
    onehot = (labels[None, :] == class_column).astype(BF16)

    half = local_centres // 2
    centres_2 = [swap(centres[:half], 2)]
    stack = jnp.concatenate([beta.T, onehot], axis=1)[None]
    far = [0]
    for mask in reversed(outer):
        stack = jnp.concatenate([stack, swap(stack, mask)])
        far = far + [offset ^ mask for offset in far]
    count = len(far)
    points_late, stack = lax.optimization_barrier((points, stack))
    onehots = stack[:, :, local_centres:]
    coeffs = stack[:, :, :local_centres]
    received = swap(coeffs, 2)
    near, distant = swap(points_late, outer[0]), swap(points_late, outer[-1])
    alpha, tri_0 = alpha_step(me, far, coeffs, tri_inverse, None, False)
    centres_late, received, near = lax.optimization_barrier((centres, received, near))
    centres_2 = centres_2 + [swap(centres_late[half:], 2)]
    near_2 = [offset ^ 2 for offset in far]
    alpha, tri_2 = alpha_step(me, near_2, received, tri_inverse, alpha, False)
    received = swap(jnp.concatenate([coeffs, received]), 1)
    received, distant = lax.optimization_barrier((received, distant))
    far_points = {0: points, outer[0]: near, outer[-1]: distant}
    for mask in outer[1:-1]:
        far_points[mask] = swap(points_late, mask)
    for offset in far:
        if offset not in far_points:
            low = offset & -offset
            far_points[offset] = swap(far_points[offset ^ low], low)
    near_13 = [offset ^ 1 for offset in far + near_2]
    alpha, tri_13 = alpha_step(me, near_13, received, tri_inverse, alpha, True)

    point_blocks = [far_points[offset] for offset in far]
    point_parts = [[at for at, offset in enumerate(far) if offset < outer[-1]]]
    point_parts = point_parts + [[at for at in range(count) if at not in point_parts[0]]]
    far_parts = [far[at] for part in point_parts for at in part]
    *centres_2, latest = lax.optimization_barrier((*centres_2, alpha))
    centres_3 = [swap(piece, 1) for piece in centres_2]
    centre_parts = [[[centres], [swap(centres, 1)]], [centres_2, centres_3]]
    tiles = []
    for part in point_parts:
        row = []
        for centre_part in centre_parts:
            latest = kernel_tile([point_blocks[at] for at in part], centre_part, latest)
            row.append(latest)
        tiles.append(row)
    alpha_2 = swap(alpha, 2)
    alpha_1 = swap(alpha, 1)
    alpha_3 = swap(alpha_2, 1)
    logit_sum = partial_logits(tiles, (alpha, alpha_1, alpha_2, alpha_3))

    block = points.shape[0]
    for mask in outer:
        received = swap(logit_sum, mask)
        order = [far_parts.index(offset ^ mask) for offset in far_parts]
        if mask != outer[-1]:
            moved = [received[:, source * block : (source + 1) * block] for source in order]
            logit_sum = logit_sum + jnp.concatenate(moved, axis=1)
    keep, send, logits = kernel_gradient(logit_sum, received, order, bias_column, onehots, [far.index(offset) for offset in far_parts], tiles)

    received = swap(send, 1)
    received_2 = swap(keep[1] + received[1], 2)
    grad = ((keep[0] + received[0] + received_2) * (1.0 / math.sqrt(total_points))).astype(BF16)

    term_3 = gradient_terms(grad, tri_13, count, count)
    received_3 = swap(term_3, 1)
    term_2 = gradient_terms(grad, tri_2, 0, count)
    received_2 = swap(term_2 + received_3, 2)
    term_1 = gradient_terms(grad, tri_13, 0, count)
    received_1 = swap(term_1, 1)
    term_0 = gradient_terms(grad, tri_0, 0, count)
    total = term_0 + received_1 + received_2
    held = list(far)
    for mask in outer:
        keep = [at for at, offset in enumerate(held) if not offset & mask]
        send = [held.index(held[at] ^ mask) for at in keep]
        received = swap(jnp.stack([total[at] for at in send]), mask)
        total = jnp.stack([total[at] for at in keep]) + received
        held = [held[at] for at in keep]
    return (total[0].T, logits.T)


def solution(mesh):
    return jax.shard_map(
        on_device,
        mesh=mesh,
        in_specs=(
            P(("groups", "pts"), None),
            P(("groups", "pts")),
            P(("groups", "pts"), None),
            P(("groups", "pts"), None),
            P(("groups", "pts"), None),
            P("groups"),
        ),
        out_specs=(P(("groups", "pts"), None), P(("groups", "pts"), None)),
        check_vma=False,
    )
```

```python
import math

import jax
import jax.numpy as jnp
from jax import lax
from jax.experimental import pallas as pl
from jax.experimental.pallas import tpu as pltpu
from jax.sharding import PartitionSpec as P

BF16 = jnp.bfloat16
F32 = jnp.float32
ROWS_BY_ROWS = (((1,), (1,)), ((), ()))
MIB = 1 << 20
IN_FLIGHT = 3


def params(mib):
    return pltpu.CompilerParams(vmem_limit_bytes=mib * MIB)


def in_vmem():
    return pl.BlockSpec(memory_space=pltpu.VMEM)


def anywhere():
    return pl.BlockSpec(memory_space=pl.ANY)


def in_smem():
    return pl.BlockSpec(memory_space=pltpu.SMEM)


def cost(flops, bytes_accessed):
    return pl.CostEstimate(flops=int(flops), bytes_accessed=int(bytes_accessed), transcendentals=0)


def alpha_sum(me, tri, brought, known, total, after):
    offsets, betas = brought
    rows = tri.shape[0]
    classes, width = betas.shape[1:]
    count = len(offsets)
    ahead = min(IN_FLIGHT, count)
    last = total is not None

    def body(me_ref, tri_ref, after_ref, beta_ref, *refs):
        known_refs, (out_ref, held_ref, sems) = refs[:-3], refs[-3:]
        copies = [
            pltpu.make_async_copy(
                tri_ref.at[:, pl.ds(pl.multiple_of((me_ref[0] ^ offset) * width, width), width)],
                held_ref.at[at],
                sems.at[at],
            )
            for at, offset in enumerate(offsets)
        ]
        for copy in copies[:ahead]:
            copy.start()
        acc = None
        if last:
            total_ref, block_ref, known_beta_ref = known_refs
            acc = total_ref[...]
            for at in range(known_beta_ref.shape[0]):
                acc = acc + lax.dot_general(
                    known_beta_ref[at], block_ref[known[1] + at], ROWS_BY_ROWS, preferred_element_type=F32
                )
        for at in range(count):
            copies[at].wait()
            if at + ahead < count:
                copies[at + ahead].start()
            if at < betas.shape[0]:
                term = lax.dot_general(beta_ref[at], held_ref[at], ROWS_BY_ROWS, preferred_element_type=F32)
                acc = term if acc is None else acc + term
        out_ref[...] = acc.astype(out_ref.dtype)

    operands = (me, tri, after, betas)
    if last:
        operands += (total, pltpu.with_memory_space_constraint(known[0], pltpu.VMEM), known[2])
    return pl.pallas_call(
        body,
        out_shape=[
            jax.ShapeDtypeStruct((classes, rows), BF16 if last else F32),
            pltpu.VMEM((count, rows, width), BF16),
        ],
        in_specs=[in_smem(), anywhere(), anywhere()] + [in_vmem()] * (len(operands) - 3),
        out_specs=[in_vmem(), in_vmem()],
        scratch_shapes=[pltpu.SemaphoreType.DMA((count,))],
        compiler_params=params(8),
        cost_estimate=cost(2 * rows * count * width * 128, 2 * rows * count * width),
        name="alpha_sum",
    )(*operands)


def gradient_terms(grad, blocks, first, count):
    classes, rows = grad.shape
    width = blocks.shape[2]

    def body(grad_ref, block_ref, out_ref):
        for at in range(count):
            out_ref[at] = jnp.dot(grad_ref[...], block_ref[first + at], preferred_element_type=F32)

    return pl.pallas_call(
        body,
        out_shape=jax.ShapeDtypeStruct((count, classes, width), F32),
        in_specs=[in_vmem(), in_vmem()],
        out_specs=in_vmem(),
        compiler_params=params(8),
        cost_estimate=cost(2 * rows * count * width * 128, 1024),
        name="gradient_terms",
    )(grad, pltpu.with_memory_space_constraint(blocks, pltpu.VMEM))


def kernel_tile(block, points, centre_blocks, after):
    count, _, features = points.shape
    local = sum(piece.shape[0] for piece in centre_blocks[0])
    factor = 1.0 / math.sqrt(features)
    pieces = [piece for pieces in centre_blocks for piece in pieces]
    total = count * block

    def body(point_ref, *refs):
        piece_refs, out_ref = refs[:-2], refs[-1]
        row = 0
        for piece_ref in piece_refs:
            which, first, rows = row // local, row % local, piece_ref.shape[0]
            for at in range(count):
                inner = lax.dot_general(
                    piece_ref[...], point_ref[at, :block], ROWS_BY_ROWS, preferred_element_type=F32
                )
                value = inner * factor + 1.0
                out_ref[which, first : first + rows, at * block : (at + 1) * block] = (
                    value * value * value
                ).astype(BF16)
            row += rows

    return pl.pallas_call(
        body,
        out_shape=pltpu.VMEM((len(centre_blocks), local, total), BF16),
        in_specs=[in_vmem()] * (1 + len(pieces)) + [anywhere()],
        out_specs=in_vmem(),
        compiler_params=params(8),
        cost_estimate=cost(2 * total * len(centre_blocks) * local * features, 1024),
        name="kernel_tile",
    )(points, *pieces, after)


def partial_logits(tiles, alphas):
    classes = alphas[0].shape[0]
    sizes = [row[0].shape[2] for row in tiles]
    flat = [tile for row in tiles for tile in row]
    counts = [tile.shape[0] for tile in tiles[0]]

    def body(*refs):
        alpha_refs, tile_refs, out_ref = refs[: len(alphas)], refs[len(alphas) : -1], refs[-1]
        for part, size in enumerate(sizes):
            first = sum(sizes[:part])
            acc = None
            index = 0
            for which, count in enumerate(counts):
                tile_ref = tile_refs[part * len(counts) + which]
                for at in range(count):
                    term = jnp.dot(alpha_refs[index][...], tile_ref[at], preferred_element_type=F32)
                    acc = term if acc is None else acc + term
                    index += 1
            out_ref[:, first : first + size] = acc

    return pl.pallas_call(
        body,
        out_shape=jax.ShapeDtypeStruct((classes, sum(sizes)), F32),
        in_specs=[in_vmem()] * (len(alphas) + len(flat)),
        out_specs=in_vmem(),
        compiler_params=params(8),
        cost_estimate=cost(2 * sum(tile.size for tile in flat) * 128, 1024),
        name="partial_logits",
    )(*alphas, *flat)


def kernel_gradient(logit_sum, received, order, bias, points, tiles):
    flat = [tile for row in tiles for tile in row]
    n_parts = len(tiles[0])
    local = flat[0].shape[1]
    sizes = [row[0].shape[2] for row in tiles]
    classes, total = logit_sum.shape
    block = total // len(order)

    def body(sum_ref, received_ref, bias_ref, *refs):
        point_refs, tile_refs = refs[: len(points)], refs[len(points) : len(points) + len(flat)]
        *out_refs, logits_ref, resid_ref = refs[len(points) + len(flat) :]
        for at, source in enumerate(order):
            here = slice(at * block, (at + 1) * block)
            there = slice(source * block, (source + 1) * block)
            logits = sum_ref[:, here] + received_ref[:, there] + bias_ref[:, :1]
            if at == 0:
                logits_ref[...] = logits
            held = point_refs[at // points[0].shape[0]]
            onehot = held[at % points[0].shape[0], block : block + classes, :block].astype(F32)
            resid_ref[:, here] = (jax.nn.sigmoid(logits) - onehot).astype(BF16)
        for parity, out_ref in enumerate(out_refs):
            for which in range(n_parts):
                acc = None
                for part, size in enumerate(sizes):
                    first = sum(sizes[:part])
                    term = lax.dot_general(
                        resid_ref[:, first : first + size],
                        tile_refs[part * n_parts + which][parity],
                        ROWS_BY_ROWS,
                        preferred_element_type=F32,
                    )
                    acc = term if acc is None else acc + term
                out_ref[which] = acc

    return pl.pallas_call(
        body,
        out_shape=[jax.ShapeDtypeStruct((n_parts, classes, local), F32)] * 2
        + [jax.ShapeDtypeStruct((classes, block), F32)],
        in_specs=[in_vmem()] * (3 + len(points) + len(flat)),
        out_specs=[in_vmem()] * 3,
        scratch_shapes=[pltpu.VMEM((classes, total), BF16)],
        compiler_params=params(8),
        cost_estimate=cost(2 * sum(tile.size for tile in flat) * 128, 1024),
        name="kernel_gradient",
    )(logit_sum, received, bias, *points, *flat)


def on_device(points, labels, centres, tri_inverse, beta, bias):
    devices = lax.axis_size("pts")
    local_centres, classes = beta.shape
    total_points = points.shape[0] * devices
    outer = [1 << bit for bit in range(2, devices.bit_length() - 1)]

    def swap(array, mask):
        return lax.ppermute(array, "pts", [(index, index ^ mask) for index in range(devices)])

    tri_inverse = pltpu.with_memory_space_constraint(tri_inverse, pltpu.HBM)
    me = lax.axis_index("pts").astype(jnp.int32).reshape(1)
    bias_column = jnp.broadcast_to(bias[:, None], (classes, 128))
    class_column = jnp.arange(classes, dtype=jnp.int32)[:, None]
    onehot = (labels[None, :] == class_column).astype(BF16)

    block, features = points.shape
    points = jnp.concatenate([points, jnp.pad(onehot, ((0, 0), (0, features - block)))])[None]
    half = local_centres // 2
    centre_halves = [centres[:half], centres[half:]]
    centres_2 = [swap(centre_halves[0], 2)]
    coeffs = beta.T[None]
    far = [0]
    for mask in reversed(outer):
        coeffs = jnp.concatenate([coeffs, swap(coeffs, mask)])
        far = far + [offset ^ mask for offset in far]
        if mask != outer[0]:
            points, coeffs = lax.optimization_barrier((points, coeffs))
            points = jnp.concatenate([points, swap(points, mask)])
    count = len(far)
    coeffs_2 = swap(coeffs, 2)
    near_2 = [offset ^ 2 for offset in far]
    near_13 = [offset ^ 1 for offset in far + near_2]
    alpha, tri_02 = alpha_sum(me, tri_inverse, (far + near_2, coeffs), None, None, coeffs)
    later, coeffs_2, alpha, centres_2[0] = lax.optimization_barrier((centre_halves[1], coeffs_2, alpha, centres_2[0]))
    centres_2.append(swap(later, 2))
    coeffs_13 = swap(jnp.concatenate([coeffs, coeffs_2]), 1)
    alpha, tri_13 = alpha_sum(me, tri_inverse, (near_13, coeffs_13), (tri_02, count, coeffs_2), alpha, points)
    points = [points, swap(points, outer[0])]

    alpha_2 = swap(alpha, 2)
    near_centres = [[centres], [swap(centres, 1)]]
    tile_00 = kernel_tile(block, points[0], near_centres, alpha)
    alpha_2, tile_00, points[1] = lax.optimization_barrier((alpha_2, tile_00, points[1]))
    alpha_1 = swap(alpha, 1)
    alpha_3 = swap(alpha_2, 1)
    *centres_2, alpha = lax.optimization_barrier((*centres_2, alpha))
    far_centres = [centres_2, [swap(piece, 1) for piece in centres_2]]
    tile_01 = kernel_tile(block, points[0], far_centres, tile_00)
    tile_10 = kernel_tile(block, points[1], near_centres, tile_01)
    tile_11 = kernel_tile(block, points[1], far_centres, tile_10)
    tiles = [[tile_00, tile_01], [tile_10, tile_11]]
    logit_sum = partial_logits(tiles, (alpha, alpha_1, alpha_2, alpha_3))

    for mask in outer:
        received = swap(logit_sum, mask)
        order = [far.index(offset ^ mask) for offset in far]
        if mask != outer[-1]:
            moved = [received[:, source * block : (source + 1) * block] for source in order]
            logit_sum = logit_sum + jnp.concatenate(moved, axis=1)
    keep, send, logits = kernel_gradient(logit_sum, received, order, bias_column, points, tiles)

    received = swap(send, 1)
    received_2 = swap(keep[1] + received[1], 2)
    grad = ((keep[0] + received[0] + received_2) * (1.0 / math.sqrt(total_points))).astype(BF16)

    term_3 = gradient_terms(grad, tri_13, count, count)
    received_3 = swap(term_3, 1)
    term_2 = gradient_terms(grad, tri_02, count, count)
    received_2 = swap(term_2 + received_3, 2)
    term_1 = gradient_terms(grad, tri_13, 0, count)
    received_1 = swap(term_1, 1)
    term_0 = gradient_terms(grad, tri_02, 0, count)
    total = term_0 + received_1 + received_2
    gradient = total[0]
    for at, offset in enumerate(far[1:], 1):
        gradient = gradient + swap(total[at], offset)
    return (gradient.T, logits.T)


def solution(mesh):
    return jax.shard_map(
        on_device,
        mesh=mesh,
        in_specs=(
            P(("groups", "pts"), None),
            P(("groups", "pts")),
            P(("groups", "pts"), None),
            P(("groups", "pts"), None),
            P(("groups", "pts"), None),
            P("groups"),
        ),
        out_specs=(P(("groups", "pts"), None), P(("groups", "pts"), None)),
        check_vma=False,
    )
```

```python
import math

import jax
import jax.numpy as jnp
from jax import lax
from jax.experimental import pallas as pl
from jax.experimental.pallas import tpu as pltpu
from jax.sharding import PartitionSpec as P

BF16 = jnp.bfloat16
F32 = jnp.float32
ROWS_BY_ROWS = (((1,), (1,)), ((), ()))
MIB = 1 << 20
IN_FLIGHT = 3


def params(mib):
    return pltpu.CompilerParams(vmem_limit_bytes=mib * MIB)


def in_vmem():
    return pl.BlockSpec(memory_space=pltpu.VMEM)


def anywhere():
    return pl.BlockSpec(memory_space=pl.ANY)


def in_smem():
    return pl.BlockSpec(memory_space=pltpu.SMEM)


def cost(flops, bytes_accessed):
    return pl.CostEstimate(flops=int(flops), bytes_accessed=int(bytes_accessed), transcendentals=0)


def alpha_sum(me, tri, brought, known, total, after):
    offsets, betas = brought
    rows = tri.shape[0]
    classes, width = betas.shape[1:]
    count = len(offsets)
    ahead = min(IN_FLIGHT, count)
    last = total is not None

    def body(me_ref, tri_ref, after_ref, beta_ref, *refs):
        known_refs, (out_ref, held_ref, sems) = refs[:-3], refs[-3:]
        copies = [
            pltpu.make_async_copy(
                tri_ref.at[:, pl.ds(pl.multiple_of((me_ref[0] ^ offset) * width, width), width)],
                held_ref.at[at],
                sems.at[at],
            )
            for at, offset in enumerate(offsets)
        ]
        for copy in copies[:ahead]:
            copy.start()
        acc = None
        if last:
            total_ref, block_ref, known_beta_ref = known_refs
            acc = total_ref[...]
            for at in range(known_beta_ref.shape[0]):
                acc = acc + lax.dot_general(
                    known_beta_ref[at], block_ref[known[1] + at], ROWS_BY_ROWS, preferred_element_type=F32
                )
        for at in range(count):
            copies[at].wait()
            if at + ahead < count:
                copies[at + ahead].start()
            if at < betas.shape[0]:
                term = lax.dot_general(beta_ref[at], held_ref[at], ROWS_BY_ROWS, preferred_element_type=F32)
                acc = term if acc is None else acc + term
        out_ref[...] = acc.astype(out_ref.dtype)

    operands = (me, tri, after, betas)
    if last:
        operands += (total, pltpu.with_memory_space_constraint(known[0], pltpu.VMEM), known[2])
    return pl.pallas_call(
        body,
        out_shape=[
            jax.ShapeDtypeStruct((classes, rows), BF16 if last else F32),
            pltpu.VMEM((count, rows, width), BF16),
        ],
        in_specs=[in_smem(), anywhere(), anywhere()] + [in_vmem()] * (len(operands) - 3),
        out_specs=[in_vmem(), in_vmem()],
        scratch_shapes=[pltpu.SemaphoreType.DMA((count,))],
        compiler_params=params(8),
        cost_estimate=cost(2 * rows * count * width * 128, 2 * rows * count * width),
        name="alpha_sum",
    )(*operands)


def gradient_terms(grad, blocks, first, count, step, after):
    classes, rows = grad.shape
    width = blocks.shape[2]

    def body(after_ref, grad_ref, block_ref, out_ref):
        for at in range(count):
            out_ref[at] = jnp.dot(grad_ref[...], block_ref[first + step * at], preferred_element_type=F32)

    return pl.pallas_call(
        body,
        out_shape=jax.ShapeDtypeStruct((count, classes, width), F32),
        in_specs=[anywhere(), in_vmem(), in_vmem()],
        out_specs=in_vmem(),
        compiler_params=params(8),
        cost_estimate=cost(2 * rows * count * width * 128, 1024),
        name="gradient_terms",
    )(after, grad, pltpu.with_memory_space_constraint(blocks, pltpu.VMEM))


def kernel_tile(block, points, centre_blocks, after):
    count, _, features = points.shape
    local = sum(piece.shape[0] for piece in centre_blocks[0])
    factor = 1.0 / math.sqrt(features)
    pieces = [piece for pieces in centre_blocks for piece in pieces]
    total = count * block

    def body(point_ref, *refs):
        piece_refs, out_ref = refs[:-2], refs[-1]
        row = 0
        for piece_ref in piece_refs:
            which, first, rows = row // local, row % local, piece_ref.shape[0]
            for at in range(count):
                inner = lax.dot_general(
                    piece_ref[...], point_ref[at, :block], ROWS_BY_ROWS, preferred_element_type=F32
                )
                value = inner * factor + 1.0
                out_ref[which, first : first + rows, at * block : (at + 1) * block] = (
                    value * value * value
                ).astype(BF16)
            row += rows

    return pl.pallas_call(
        body,
        out_shape=pltpu.VMEM((len(centre_blocks), local, total), BF16),
        in_specs=[in_vmem()] * (1 + len(pieces)) + [anywhere()],
        out_specs=in_vmem(),
        compiler_params=params(8),
        cost_estimate=cost(2 * total * len(centre_blocks) * local * features, 1024),
        name="kernel_tile",
    )(points, *pieces, after)


def partial_logits(tiles, alphas):
    classes = alphas[0].shape[0]
    sizes = [row[0].shape[2] for row in tiles]
    flat = [tile for row in tiles for tile in row]
    counts = [tile.shape[0] for tile in tiles[0]]

    def body(*refs):
        alpha_refs, tile_refs, out_ref = refs[: len(alphas)], refs[len(alphas) : -1], refs[-1]
        for part, size in enumerate(sizes):
            first = sum(sizes[:part])
            acc = None
            index = 0
            for which, count in enumerate(counts):
                tile_ref = tile_refs[part * len(counts) + which]
                for at in range(count):
                    term = jnp.dot(alpha_refs[index][...], tile_ref[at], preferred_element_type=F32)
                    acc = term if acc is None else acc + term
                    index += 1
            out_ref[:, first : first + size] = acc

    return pl.pallas_call(
        body,
        out_shape=jax.ShapeDtypeStruct((classes, sum(sizes)), F32),
        in_specs=[in_vmem()] * (len(alphas) + len(flat)),
        out_specs=in_vmem(),
        compiler_params=params(8),
        cost_estimate=cost(2 * sum(tile.size for tile in flat) * 128, 1024),
        name="partial_logits",
    )(*alphas, *flat)


def residual(logit_sum, received, order, bias, points):
    classes, total = logit_sum.shape
    block = total // len(order)
    blocks = [(which, at) for which, array in enumerate(points) for at in range(array.shape[0])]

    def compute(sum_ref, received_ref, bias_ref, point_refs, logits_ref, resid_ref):
        for at, source in enumerate(order):
            here = slice(at * block, (at + 1) * block)
            there = slice(source * block, (source + 1) * block)
            logits = sum_ref[:, here] + received_ref[:, there] + bias_ref[:, :1]
            if at == 0:
                logits_ref[...] = logits
            which, row = blocks[at]
            onehot = point_refs[which][row, block : block + classes, :block].astype(F32)
            resid_ref[:, here] = (jax.nn.sigmoid(logits) - onehot).astype(BF16)

    return compute


def kernel_gradient(parity, resid, tiles, residual_of=None):
    flat = [tile for row in tiles for tile in row]
    n_parts = len(tiles[0])
    local = flat[0].shape[1]
    sizes = [row[0].shape[2] for row in tiles]
    total = sum(sizes)
    out_shape = []
    if residual_of is None:
        operands = [resid]
    else:
        compute, (logit_sum, received, bias, points) = residual_of
        operands = [logit_sum, received, bias, *points]
        block = points[0].shape[1] - logit_sum.shape[0]
        out_shape = [jax.ShapeDtypeStruct((logit_sum.shape[0], block), F32)]
        out_shape.append(jax.ShapeDtypeStruct(logit_sum.shape, BF16))
    classes = operands[0].shape[0]
    n_operands = len(operands)

    def body(*refs):
        tile_refs = refs[n_operands : n_operands + len(flat)]
        out_ref, *more_refs = refs[n_operands + len(flat) :]
        resid_ref = refs[0]
        if residual_of is not None:
            logits_ref, resid_ref = more_refs
            compute(*refs[:3], refs[3:n_operands], logits_ref, resid_ref)
        for which in range(n_parts):
            acc = None
            for part, size in enumerate(sizes):
                first = sum(sizes[:part])
                term = lax.dot_general(
                    resid_ref[:, first : first + size],
                    tile_refs[part * n_parts + which][parity],
                    ROWS_BY_ROWS,
                    preferred_element_type=F32,
                )
                acc = term if acc is None else acc + term
            out_ref[which] = acc

    return pl.pallas_call(
        body,
        out_shape=[jax.ShapeDtypeStruct((n_parts, classes, local), F32)] + out_shape,
        in_specs=[in_vmem()] * (n_operands + len(flat)),
        out_specs=[in_vmem()] * (1 + len(out_shape)),
        compiler_params=params(8),
        cost_estimate=cost(2 * total * n_parts * local * 128, 1024),
        name="kernel_gradient",
    )(*operands, *flat)


def on_device(points, labels, centres, tri_inverse, beta, bias):
    devices = lax.axis_size("pts")
    local_centres, classes = beta.shape
    total_points = points.shape[0] * devices
    outer = [1 << bit for bit in range(2, devices.bit_length() - 1)]

    def swap(array, mask):
        return lax.ppermute(array, "pts", [(index, index ^ mask) for index in range(devices)])

    tri_inverse = pltpu.with_memory_space_constraint(tri_inverse, pltpu.HBM)
    me = lax.axis_index("pts").astype(jnp.int32).reshape(1)
    bias_column = jnp.broadcast_to(bias[:, None], (classes, 128))
    class_column = jnp.arange(classes, dtype=jnp.int32)[:, None]
    onehot = (labels[None, :] == class_column).astype(BF16)

    block, features = points.shape
    points = jnp.concatenate([points, jnp.pad(onehot, ((0, 0), (0, features - block)))])[None]
    half = local_centres * 1//2
    centre_halves = [centres[:half], centres[half:]]
    centres_2 = [swap(centre_halves[0], 2)]
    coeffs = beta.T[None]
    far = [0]
    for mask in reversed(outer):
        coeffs = jnp.concatenate([coeffs, swap(coeffs, mask)])
        far = far + [offset ^ mask for offset in far]
        if mask != outer[0]:
            points, coeffs = lax.optimization_barrier((points, coeffs))
            points = jnp.concatenate([points, swap(points, mask)])
    count = len(far)
    later, coeffs = lax.optimization_barrier((centre_halves[1], coeffs))
    coeffs_2 = swap(coeffs, 2)
    centres_2.append(swap(later, 2))
    near_2 = [offset ^ 2 for offset in far]
    near_13 = [offset ^ 1 for offset in far + near_2]
    alpha, tri_02 = alpha_sum(me, tri_inverse, (far + near_2, coeffs), None, None, coeffs)
    coeffs_2, alpha, centres_2[0] = lax.optimization_barrier((coeffs_2, alpha, centres_2[0]))
    coeffs_13 = swap(jnp.concatenate([coeffs, coeffs_2]), 1)
    alpha, tri_13 = alpha_sum(me, tri_inverse, (near_13, coeffs_13), (tri_02, count, coeffs_2), alpha, points)
    points = [points, swap(points, outer[0])]

    alpha_2 = swap(alpha, 2)
    near_centres = [[centres], [swap(centres, 1)]]
    tile_00 = kernel_tile(block, points[0], near_centres, alpha)
    alpha_2, tile_00, points[1] = lax.optimization_barrier((alpha_2, tile_00, points[1]))
    alpha_1 = swap(alpha, 1)
    alpha_3 = swap(alpha_2, 1)
    *centres_2, alpha = lax.optimization_barrier((*centres_2, alpha))
    far_centres = [centres_2, [swap(piece, 1) for piece in centres_2]]
    tile_01 = kernel_tile(block, points[0], far_centres, tile_00)
    tile_10 = kernel_tile(block, points[1], near_centres, tile_01)
    tile_11 = kernel_tile(block, points[1], far_centres, tile_10)
    tiles = [[tile_00, tile_01], [tile_10, tile_11]]
    logit_sum = partial_logits(tiles, (alpha, alpha_1, alpha_2, alpha_3))

    for mask in outer:
        received = swap(logit_sum, mask)
        order = [far.index(offset ^ mask) for offset in far]
        if mask != outer[-1]:
            moved = [received[:, source * block : (source + 1) * block] for source in order]
            logit_sum = logit_sum + jnp.concatenate(moved, axis=1)
    compute = residual(logit_sum, received, order, bias_column, points)
    send, logits, resid = kernel_gradient(1, None, tiles, (compute, (logit_sum, received, bias_column, points)))
    received = swap(send, 1)
    (keep,) = kernel_gradient(0, resid, tiles)

    received_2 = swap(keep[1] + received[1], 2)
    grad = ((keep[0] + received[0] + received_2) * (1.0 / math.sqrt(total_points))).astype(BF16)

    half = count // 2
    position = {offset: at for at, offset in enumerate(far)}
    near_first = sorted(far, key=lambda offset: (offset & outer[-1], position[offset]))
    latest = grad
    sums = {}
    for offsets in (near_first[half:], near_first[:half]):
        at = position[offsets[0]]
        step = position[offsets[1]] - at if half > 1 else 1
        parts = []
        for held, first in ((tri_13, count), (tri_02, count), (tri_13, 0), (tri_02, 0)):
            parts.append((held, first + at))
        term_3 = gradient_terms(grad, *parts[0], half, step, latest)
        received_3 = swap(term_3, 1)
        term_2 = gradient_terms(grad, *parts[1], half, step, term_3)
        ahead = term_2 + received_3
        received_2 = swap(ahead, 2)
        term_1 = gradient_terms(grad, *parts[2], half, step, ahead)
        received_1 = swap(term_1, 1)
        latest = gradient_terms(grad, *parts[3], half, step, term_1)
        total = latest + received_1 + received_2
        for index, offset in enumerate(offsets):
            sums[offset] = total[index]
    gradient = sums[0]
    for offset in reversed(near_first[1:]):
        gradient = gradient + swap(sums[offset], offset)
    return (gradient.T, logits.T)


def solution(mesh):
    return jax.shard_map(
        on_device,
        mesh=mesh,
        in_specs=(
            P(("groups", "pts"), None),
            P(("groups", "pts")),
            P(("groups", "pts"), None),
            P(("groups", "pts"), None),
            P(("groups", "pts"), None),
            P("groups"),
        ),
        out_specs=(P(("groups", "pts"), None), P(("groups", "pts"), None)),
        check_vma=False,
    )
```

```python
import math

import jax
import jax.numpy as jnp
from jax import lax
from jax.experimental import pallas as pl
from jax.experimental.pallas import tpu as pltpu
from jax.sharding import PartitionSpec as P

BF16 = jnp.bfloat16
F32 = jnp.float32
ROWS_BY_ROWS = (((1,), (1,)), ((), ()))
MIB = 1 << 20
IN_FLIGHT = 3


def params(mib):
    return pltpu.CompilerParams(vmem_limit_bytes=mib * MIB)


def in_hbm(array):
    return pltpu.with_memory_space_constraint(array, pltpu.HBM)


def in_vmem():
    return pl.BlockSpec(memory_space=pltpu.VMEM)


def anywhere():
    return pl.BlockSpec(memory_space=pl.ANY)


def in_smem():
    return pl.BlockSpec(memory_space=pltpu.SMEM)


def cost(flops, bytes_accessed):
    return pl.CostEstimate(flops=int(flops), bytes_accessed=int(bytes_accessed), transcendentals=0)


def alpha_sum(me, tri, brought, known, total, after):
    offsets, betas = brought
    rows = tri.shape[0]
    classes, width = betas.shape[1:]
    count = len(offsets)
    ahead = min(IN_FLIGHT, count)
    last = total is not None

    def body(me_ref, tri_ref, after_ref, beta_ref, *refs):
        known_refs, (out_ref, held_ref, sems) = refs[:-3], refs[-3:]
        copies = [
            pltpu.make_async_copy(
                tri_ref.at[:, pl.ds(pl.multiple_of((me_ref[0] ^ offset) * width, width), width)],
                held_ref.at[at],
                sems.at[at],
            )
            for at, offset in enumerate(offsets)
        ]
        for copy in copies[:ahead]:
            copy.start()
        acc = None
        if last:
            total_ref, block_ref, known_beta_ref = known_refs
            acc = total_ref[...]
            for at in range(known_beta_ref.shape[0]):
                acc = acc + lax.dot_general(
                    known_beta_ref[at], block_ref[known[1] + at], ROWS_BY_ROWS, preferred_element_type=F32
                )
        for at in range(count):
            copies[at].wait()
            if at + ahead < count:
                copies[at + ahead].start()
            if at < betas.shape[0]:
                term = lax.dot_general(beta_ref[at], held_ref[at], ROWS_BY_ROWS, preferred_element_type=F32)
                acc = term if acc is None else acc + term
        out_ref[...] = acc.astype(out_ref.dtype)

    operands = (me, tri, after, betas)
    if last:
        operands += (total, pltpu.with_memory_space_constraint(known[0], pltpu.VMEM), known[2])
    return pl.pallas_call(
        body,
        out_shape=[
            jax.ShapeDtypeStruct((classes, rows), BF16 if last else F32),
            pltpu.VMEM((count, rows, width), BF16),
        ],
        in_specs=[in_smem(), anywhere(), anywhere()] + [in_vmem()] * (len(operands) - 3),
        out_specs=[in_vmem(), in_vmem()],
        scratch_shapes=[pltpu.SemaphoreType.DMA((count,))],
        compiler_params=params(8),
        cost_estimate=cost(2 * rows * count * width * 128, 2 * rows * count * width),
        name="alpha_sum",
    )(*operands)


def prepare(points, labels, centres, beta):
    half = centres.shape[0] // 2
    block, features = points.shape
    classes = beta.shape[0]

    def body(points_ref, labels_ref, centres_ref, beta_ref, ext_ref, first_ref, second_ref, held_ref, row_ref, sems):
        moves = (
            (labels_ref, row_ref),
            (centres_ref.at[pl.ds(0, half)], first_ref),
            (points_ref, ext_ref.at[0, pl.ds(0, block)]),
            (beta_ref, held_ref.at[0]),
            (centres_ref.at[pl.ds(half, half)], second_ref),
        )
        copies = [pltpu.make_async_copy(source, target, sems.at[at]) for at, (source, target) in enumerate(moves)]
        for copy in copies:
            copy.start()
        class_column = lax.broadcasted_iota(jnp.int32, (classes, block), 0)
        ext_ref[0, block:, :] = jnp.zeros((classes, features), BF16)
        copies[0].wait()
        ext_ref[0, block:, :block] = jnp.where(row_ref[...] == class_column, 1.0, 0.0).astype(BF16)
        for copy in copies[1:]:
            copy.wait()

    return pl.pallas_call(
        body,
        out_shape=[
            pltpu.VMEM((1, block + classes, features), BF16),
            pltpu.VMEM((half, features), BF16),
            pltpu.VMEM((half, features), BF16),
            pltpu.VMEM((1, *beta.shape), BF16),
        ],
        in_specs=[anywhere()] * 4,
        out_specs=[in_vmem()] * 4,
        scratch_shapes=[pltpu.VMEM((1, block), jnp.int32), pltpu.SemaphoreType.DMA((5,))],
        compiler_params=params(8),
        cost_estimate=cost(1024, 4 * centres.size),
        name="prepare",
    )(in_hbm(points), in_hbm(labels[None, :]), in_hbm(centres), in_hbm(beta))


def gradient_terms(grad, blocks, first, count, after):
    classes, rows = grad.shape
    width = blocks.shape[2]

    def body(after_ref, grad_ref, block_ref, out_ref):
        for at in range(count):
            out_ref[at] = jnp.dot(grad_ref[...], block_ref[first + at], preferred_element_type=F32)

    return pl.pallas_call(
        body,
        out_shape=jax.ShapeDtypeStruct((count, classes, width), F32),
        in_specs=[anywhere(), in_vmem(), in_vmem()],
        out_specs=in_vmem(),
        compiler_params=params(8),
        cost_estimate=cost(2 * rows * count * width * 128, 1024),
        name="gradient_terms",
    )(after, grad, pltpu.with_memory_space_constraint(blocks, pltpu.VMEM))


def kernel_tile(block, points, centre_blocks, after):
    count, _, features = points.shape
    local = sum(piece.shape[0] for piece in centre_blocks[0])
    factor = 1.0 / math.sqrt(features)
    pieces = [piece for pieces in centre_blocks for piece in pieces]
    total = count * block

    def body(point_ref, *refs):
        piece_refs, out_ref = refs[:-2], refs[-1]
        row = 0
        for piece_ref in piece_refs:
            which, first, rows = row // local, row % local, piece_ref.shape[0]
            for at in range(count):
                inner = lax.dot_general(
                    piece_ref[...], point_ref[at, :block], ROWS_BY_ROWS, preferred_element_type=F32
                )
                value = inner * factor + 1.0
                out_ref[which, first : first + rows, at * block : (at + 1) * block] = (
                    value * value * value
                ).astype(BF16)
            row += rows

    return pl.pallas_call(
        body,
        out_shape=pltpu.VMEM((len(centre_blocks), local, total), BF16),
        in_specs=[in_vmem()] * (1 + len(pieces)) + [anywhere()],
        out_specs=in_vmem(),
        compiler_params=params(8),
        cost_estimate=cost(1024, 1024),
        name="kernel_tile",
    )(points, *pieces, after)


def partial_logits(tiles, alphas):
    classes = alphas[0].shape[0]
    sizes = [row[0].shape[2] for row in tiles]
    flat = [tile for row in tiles for tile in row]
    counts = [tile.shape[0] for tile in tiles[0]]

    def body(*refs):
        alpha_refs, tile_refs, out_ref = refs[: len(alphas)], refs[len(alphas) : -1], refs[-1]
        for part, size in enumerate(sizes):
            first = sum(sizes[:part])
            acc = None
            index = 0
            for which, count in enumerate(counts):
                tile_ref = tile_refs[part * len(counts) + which]
                for at in range(count):
                    term = jnp.dot(alpha_refs[index][...], tile_ref[at], preferred_element_type=F32)
                    acc = term if acc is None else acc + term
                    index += 1
            out_ref[:, first : first + size] = acc

    return pl.pallas_call(
        body,
        out_shape=jax.ShapeDtypeStruct((classes, sum(sizes)), F32),
        in_specs=[in_vmem()] * (len(alphas) + len(flat)),
        out_specs=in_vmem(),
        compiler_params=params(8),
        cost_estimate=cost(2 * sum(tile.size for tile in flat) * 128, 1024),
        name="partial_logits",
    )(*alphas, *flat)


def residual(logit_sum, received, orders, bias, points):
    classes, total = logit_sum.shape
    block = total // len(orders[0])
    blocks = [(which, at) for which, array in enumerate(points) for at in range(array.shape[0])]

    def compute(sum_ref, bias_ref, received_refs, point_refs, logits_ref, resid_ref):
        for at in range(len(blocks)):
            here = slice(at * block, (at + 1) * block)
            logits = sum_ref[:, here]
            for received_ref, order in zip(received_refs, orders):
                there = slice(order[at] * block, (order[at] + 1) * block)
                logits = logits + received_ref[:, there].astype(F32)
            logits = logits + bias_ref[:, :1]
            if at == 0:
                logits_ref[...] = logits
            which, row = blocks[at]
            onehot = point_refs[which][row, block : block + classes, :block].astype(F32)
            resid_ref[:, here] = (jax.nn.sigmoid(logits) - onehot).astype(BF16)

    return compute


def kernel_gradient(parity, resid, tiles, residual_of=None):
    flat = [tile for row in tiles for tile in row]
    n_parts = len(tiles[0])
    local = flat[0].shape[1]
    sizes = [row[0].shape[2] for row in tiles]
    total = sum(sizes)
    out_shape = []
    if residual_of is None:
        operands = [resid]
    else:
        compute, (logit_sum, received, bias, points) = residual_of
        operands = [logit_sum, bias, *received, *points]
        n_first = 2 + len(received)
        block = points[0].shape[1] - logit_sum.shape[0]
        out_shape = [jax.ShapeDtypeStruct((logit_sum.shape[0], block), F32)]
        out_shape.append(jax.ShapeDtypeStruct(logit_sum.shape, BF16))
    classes = operands[0].shape[0]
    n_operands = len(operands)

    def body(*refs):
        tile_refs = refs[n_operands : n_operands + len(flat)]
        out_ref, *more_refs = refs[n_operands + len(flat) :]
        resid_ref = refs[0]
        if residual_of is not None:
            logits_ref, resid_ref = more_refs
            compute(*refs[:2], refs[2:n_first], refs[n_first:n_operands], logits_ref, resid_ref)
        for which in range(n_parts):
            acc = None
            for part, size in enumerate(sizes):
                first = sum(sizes[:part])
                term = lax.dot_general(
                    resid_ref[:, first : first + size],
                    tile_refs[part * n_parts + which][parity],
                    ROWS_BY_ROWS,
                    preferred_element_type=F32,
                )
                acc = term if acc is None else acc + term
            out_ref[which] = acc

    return pl.pallas_call(
        body,
        out_shape=[jax.ShapeDtypeStruct((n_parts, classes, local), F32)] + out_shape,
        in_specs=[in_vmem()] * (n_operands + len(flat)),
        out_specs=[in_vmem()] * (1 + len(out_shape)),
        compiler_params=params(8),
        cost_estimate=cost(2 * total * n_parts * local * 128, 1024),
        name="kernel_gradient",
    )(*operands, *flat)


def on_device(points, labels, centres, tri_inverse, beta, bias):
    devices = lax.axis_size("pts")
    local_centres, classes = beta.shape
    total_points = points.shape[0] * devices
    outer = [1 << bit for bit in range(2, devices.bit_length() - 1)]

    def swap(array, mask):
        return lax.ppermute(array, "pts", [(index, index ^ mask) for index in range(devices)])

    tri_inverse = in_hbm(tri_inverse)
    me = lax.axis_index("pts").astype(jnp.int32).reshape(1)
    bias_column = jnp.broadcast_to(bias[:, None], (classes, 128))

    block = points.shape[0]
    coeffs = beta.T
    crossed = swap(coeffs[None], outer[-1])
    points, *centre_halves, coeffs = prepare(points, labels, centres, coeffs)
    centres_2 = [swap(centre_halves[0], 2)]
    far = [0]
    for mask in reversed(outer):
        coeffs = jnp.concatenate([coeffs, crossed if mask == outer[-1] else swap(coeffs, mask)])
        far = far + [offset ^ mask for offset in far]
        if mask != outer[0]:
            points, coeffs = lax.optimization_barrier((points, coeffs))
            points = jnp.concatenate([points, swap(points, mask)])
    count = len(far)
    later, coeffs = lax.optimization_barrier((centre_halves[1], coeffs))
    coeffs_2 = swap(coeffs, 2)
    centres_2.append(swap(later, 2))
    near_2 = [offset ^ 2 for offset in far]
    near_13 = [offset ^ 1 for offset in far + near_2]
    alpha, tri_02 = alpha_sum(me, tri_inverse, (far + near_2, coeffs), None, None, coeffs)
    coeffs_2, alpha, centres_2[0] = lax.optimization_barrier((coeffs_2, alpha, centres_2[0]))
    coeffs_13 = swap(jnp.concatenate([coeffs, coeffs_2]), 1)
    alpha, tri_13 = alpha_sum(me, tri_inverse, (near_13, coeffs_13), (tri_02, count, coeffs_2), alpha, points)
    points = [points, swap(points, outer[0])]

    alpha_2 = swap(alpha, 2)
    near_centres = [[centres], [swap(centres, 1)]]
    tile_00 = kernel_tile(block, points[0], near_centres, alpha)
    alpha_1 = swap(alpha, 1)
    *centres_2, alpha = lax.optimization_barrier((*centres_2, alpha))
    far_centres = [centres_2, [swap(piece, 1) for piece in centres_2]]
    tile_01 = kernel_tile(block, points[0], far_centres, tile_00)
    alpha_2, tile_01, points[1] = lax.optimization_barrier((alpha_2, tile_01, points[1]))
    alpha_3 = swap(alpha_2, 1)
    tile_10 = kernel_tile(block, points[1], near_centres, tile_01)
    tile_11 = kernel_tile(block, points[1], far_centres, tile_10)
    tiles = [[tile_00, tile_01], [tile_10, tile_11]]
    logit_sum = partial_logits(tiles, (alpha, alpha_1, alpha_2, alpha_3))

    rounded = logit_sum.astype(BF16)
    received = [swap(rounded, offset) for offset in far[1:]]
    orders = [[far.index(held ^ offset) for held in far] for offset in far[1:]]
    compute = residual(logit_sum, received, orders, bias_column, points)
    send, logits, resid = kernel_gradient(1, None, tiles, (compute, (logit_sum, received, bias_column, points)))
    received = swap(send, 1)
    (keep,) = kernel_gradient(0, resid, tiles)

    received_2 = swap(keep[1] + received[1], 2)
    grad = ((keep[0] + received[0] + received_2) * (1.0 / math.sqrt(total_points))).astype(BF16)

    term_3 = gradient_terms(grad, tri_13, count, count, grad)
    received_3 = swap(term_3, 1)
    term_1 = gradient_terms(grad, tri_13, 0, count, term_3)
    received_1 = swap(term_1, 1)
    term_2 = gradient_terms(grad, tri_02, count, count, term_1)
    ahead = (term_2 + received_3).astype(BF16)
    received_2 = swap(ahead, 2)
    term_0 = gradient_terms(grad, tri_02, 0, count, ahead)
    total = term_0 + received_1 + received_2.astype(F32)
    gradient = total[0]
    for at, offset in reversed(list(enumerate(far))[1:]):
        gradient = gradient + swap(total[at].astype(BF16), offset).astype(F32)
    return (gradient.T, logits.T)


def solution(mesh):
    return jax.shard_map(
        on_device,
        mesh=mesh,
        in_specs=(
            P(("groups", "pts"), None),
            P(("groups", "pts")),
            P(("groups", "pts"), None),
            P(("groups", "pts"), None),
            P(("groups", "pts"), None),
            P("groups"),
        ),
        out_specs=(P(("groups", "pts"), None), P(("groups", "pts"), None)),
        check_vma=False,
    )
```

```python
import math

import jax
import jax.numpy as jnp
from jax import lax
from jax.experimental import pallas as pl
from jax.experimental.pallas import tpu as pltpu
from jax.sharding import PartitionSpec as P

BF16 = jnp.bfloat16
F32 = jnp.float32
ROWS_BY_ROWS = (((1,), (1,)), ((), ()))
MIB = 1 << 20
IN_FLIGHT = 3


def params(mib):
    return pltpu.CompilerParams(vmem_limit_bytes=mib * MIB)


def in_hbm(array):
    return pltpu.with_memory_space_constraint(array, pltpu.HBM)


def in_vmem():
    return pl.BlockSpec(memory_space=pltpu.VMEM)


def anywhere():
    return pl.BlockSpec(memory_space=pl.ANY)


def in_smem():
    return pl.BlockSpec(memory_space=pltpu.SMEM)


def cost(flops, bytes_accessed):
    return pl.CostEstimate(flops=int(flops), bytes_accessed=int(bytes_accessed), transcendentals=0)


def alpha_sum(me, tri, brought, known, total, after):
    offsets, betas = brought
    rows = tri.shape[0]
    classes, width = betas.shape[1:]
    count = len(offsets)
    ahead = min(IN_FLIGHT, count)
    last = total is not None

    def body(me_ref, tri_ref, after_ref, beta_ref, *refs):
        known_refs, (out_ref, held_ref, sems) = refs[:-3], refs[-3:]
        copies = [
            pltpu.make_async_copy(
                tri_ref.at[:, pl.ds(pl.multiple_of((me_ref[0] ^ offset) * width, width), width)],
                held_ref.at[at],
                sems.at[at],
            )
            for at, offset in enumerate(offsets)
        ]
        for copy in copies[:ahead]:
            copy.start()
        acc = None
        if last:
            total_ref, block_ref, known_beta_ref = known_refs
            acc = total_ref[...]
            for at in range(known_beta_ref.shape[0]):
                acc = acc + lax.dot_general(
                    known_beta_ref[at], block_ref[known[1] + at], ROWS_BY_ROWS, preferred_element_type=F32
                )
        for at in range(count):
            copies[at].wait()
            if at + ahead < count:
                copies[at + ahead].start()
            if at < betas.shape[0]:
                term = lax.dot_general(beta_ref[at], held_ref[at], ROWS_BY_ROWS, preferred_element_type=F32)
                acc = term if acc is None else acc + term
        out_ref[...] = acc.astype(out_ref.dtype)

    operands = (me, tri, after, betas)
    if last:
        operands += (total, pltpu.with_memory_space_constraint(known[0], pltpu.VMEM), known[2])
    return pl.pallas_call(
        body,
        out_shape=[
            jax.ShapeDtypeStruct((classes, rows), BF16 if last else F32),
            pltpu.VMEM((count, rows, width), BF16),
        ],
        in_specs=[in_smem(), anywhere(), anywhere()] + [in_vmem()] * (len(operands) - 3),
        out_specs=[in_vmem(), in_vmem()],
        scratch_shapes=[pltpu.SemaphoreType.DMA((count,))],
        compiler_params=params(8),
        cost_estimate=cost(2 * rows * count * width * 128, 2 * rows * count * width),
        name="alpha_sum",
    )(*operands)


def prepare(points, labels, centres, beta):
    half = centres.shape[0] // 2
    block, features = points.shape
    classes = beta.shape[0]

    def body(points_ref, labels_ref, centres_ref, beta_ref, ext_ref, first_ref, second_ref, held_ref, row_ref, sems):
        moves = (
            (labels_ref, row_ref),
            (centres_ref.at[pl.ds(0, half)], first_ref),
            (points_ref, ext_ref.at[0, pl.ds(0, block)]),
            (beta_ref, held_ref.at[0]),
            (centres_ref.at[pl.ds(half, half)], second_ref),
        )
        copies = [pltpu.make_async_copy(source, target, sems.at[at]) for at, (source, target) in enumerate(moves)]
        for copy in copies:
            copy.start()
        class_column = lax.broadcasted_iota(jnp.int32, (classes, block), 0)
        ext_ref[0, block:, :] = jnp.zeros((classes, features), BF16)
        copies[0].wait()
        ext_ref[0, block:, :block] = jnp.where(row_ref[...] == class_column, 1.0, 0.0).astype(BF16)
        for copy in copies[1:]:
            copy.wait()

    return pl.pallas_call(
        body,
        out_shape=[
            pltpu.VMEM((1, block + classes, features), BF16),
            pltpu.VMEM((half, features), BF16),
            pltpu.VMEM((half, features), BF16),
            pltpu.VMEM((1, *beta.shape), BF16),
        ],
        in_specs=[anywhere()] * 4,
        out_specs=[in_vmem()] * 4,
        scratch_shapes=[pltpu.VMEM((1, block), jnp.int32), pltpu.SemaphoreType.DMA((5,))],
        compiler_params=params(8),
        cost_estimate=cost(1024, 4 * centres.size),
        name="prepare",
    )(in_hbm(points), in_hbm(labels[None, :]), in_hbm(centres), in_hbm(beta))


def gradient_terms(grad, blocks, first, count, after):
    classes, rows = grad.shape
    width = blocks.shape[2]

    def body(after_ref, grad_ref, block_ref, out_ref):
        for at in range(count):
            out_ref[at] = jnp.dot(grad_ref[...], block_ref[first + at], preferred_element_type=F32)

    return pl.pallas_call(
        body,
        out_shape=jax.ShapeDtypeStruct((count, classes, width), F32),
        in_specs=[anywhere(), in_vmem(), in_vmem()],
        out_specs=in_vmem(),
        compiler_params=params(8),
        cost_estimate=cost(2 * rows * count * width * 128, 1024),
        name="gradient_terms",
    )(after, grad, pltpu.with_memory_space_constraint(blocks, pltpu.VMEM))


def kernel_tile(block, points, centre_blocks, after):
    count, _, features = points.shape
    local = sum(piece.shape[0] for piece in centre_blocks[0])
    factor = 1.0 / math.sqrt(features)
    pieces = [piece for pieces in centre_blocks for piece in pieces]
    total = count * block

    def body(point_ref, *refs):
        piece_refs, out_ref = refs[:-2], refs[-1]
        row = 0
        for piece_ref in piece_refs:
            which, first, rows = row // local, row % local, piece_ref.shape[0]
            for at in range(count):
                inner = lax.dot_general(
                    piece_ref[...], point_ref[at, :block], ROWS_BY_ROWS, preferred_element_type=F32
                )
                value = inner * factor + 1.0
                out_ref[which, first : first + rows, at * block : (at + 1) * block] = (
                    value * value * value
                ).astype(BF16)
            row += rows

    return pl.pallas_call(
        body,
        out_shape=pltpu.VMEM((len(centre_blocks), local, total), BF16),
        in_specs=[in_vmem()] * (1 + len(pieces)) + [anywhere()],
        out_specs=in_vmem(),
        compiler_params=params(8),
        cost_estimate=cost(1024, 1024),
        name="kernel_tile",
    )(points, *pieces, after)


def partial_logits(tiles, alphas):
    classes = alphas[0].shape[0]
    sizes = [row[0].shape[2] for row in tiles]
    flat = [tile for row in tiles for tile in row]
    counts = [tile.shape[0] for tile in tiles[0]]

    def body(*refs):
        alpha_refs, tile_refs, out_ref = refs[: len(alphas)], refs[len(alphas) : -1], refs[-1]
        for part, size in enumerate(sizes):
            first = sum(sizes[:part])
            acc = None
            index = 0
            for which, count in enumerate(counts):
                tile_ref = tile_refs[part * len(counts) + which]
                for at in range(count):
                    term = jnp.dot(alpha_refs[index][...], tile_ref[at], preferred_element_type=F32)
                    acc = term if acc is None else acc + term
                    index += 1
            out_ref[:, first : first + size] = acc

    return pl.pallas_call(
        body,
        out_shape=jax.ShapeDtypeStruct((classes, sum(sizes)), F32),
        in_specs=[in_vmem()] * (len(alphas) + len(flat)),
        out_specs=in_vmem(),
        compiler_params=params(8),
        cost_estimate=cost(2 * sum(tile.size for tile in flat) * 128, 1024),
        name="partial_logits",
    )(*alphas, *flat)


def residual(logit_sum, received, orders, bias, points):
    classes, total = logit_sum.shape
    block = total // len(orders[0])
    blocks = [(which, at) for which, array in enumerate(points) for at in range(array.shape[0])]

    def compute(sum_ref, bias_ref, received_refs, point_refs, logits_ref, resid_ref):
        for at in range(len(blocks)):
            here = slice(at * block, (at + 1) * block)
            logits = sum_ref[:, here]
            for received_ref, order in zip(received_refs, orders):
                there = slice(order[at] * block, (order[at] + 1) * block)
                logits = logits + received_ref[:, there].astype(F32)
            logits = logits + bias_ref[:, :1]
            if at == 0:
                logits_ref[...] = logits
            which, row = blocks[at]
            onehot = point_refs[which][row, block : block + classes, :block].astype(F32)
            resid_ref[:, here] = (jax.nn.sigmoid(logits) - onehot).astype(BF16)

    return compute


def kernel_gradient(parity, resid, tiles, residual_of=None):
    flat = [tile for row in tiles for tile in row]
    n_parts = len(tiles[0])
    local = flat[0].shape[1]
    sizes = [row[0].shape[2] for row in tiles]
    total = sum(sizes)
    out_shape = []
    if residual_of is None:
        operands = [resid]
    else:
        compute, (logit_sum, received, bias, points) = residual_of
        operands = [logit_sum, bias, *received, *points]
        n_first = 2 + len(received)
        block = points[0].shape[1] - logit_sum.shape[0]
        out_shape = [jax.ShapeDtypeStruct((logit_sum.shape[0], block), F32)]
        out_shape.append(jax.ShapeDtypeStruct(logit_sum.shape, BF16))
    classes = operands[0].shape[0]
    n_operands = len(operands)

    def body(*refs):
        tile_refs = refs[n_operands : n_operands + len(flat)]
        out_ref, *more_refs = refs[n_operands + len(flat) :]
        resid_ref = refs[0]
        if residual_of is not None:
            logits_ref, resid_ref = more_refs
            compute(*refs[:2], refs[2:n_first], refs[n_first:n_operands], logits_ref, resid_ref)
        for which in range(n_parts):
            acc = None
            for part, size in enumerate(sizes):
                first = sum(sizes[:part])
                term = lax.dot_general(
                    resid_ref[:, first : first + size],
                    tile_refs[part * n_parts + which][parity],
                    ROWS_BY_ROWS,
                    preferred_element_type=F32,
                )
                acc = term if acc is None else acc + term
            out_ref[which] = acc

    return pl.pallas_call(
        body,
        out_shape=[jax.ShapeDtypeStruct((n_parts, classes, local), F32)] + out_shape,
        in_specs=[in_vmem()] * (n_operands + len(flat)),
        out_specs=[in_vmem()] * (1 + len(out_shape)),
        compiler_params=params(8),
        cost_estimate=cost(2 * total * n_parts * local * 128, 1024),
        name="kernel_gradient",
    )(*operands, *flat)


def on_device(points, labels, centres, tri_inverse, beta, bias):
    devices = lax.axis_size("pts")
    local_centres, classes = beta.shape
    total_points = points.shape[0] * devices
    outer = [1 << bit for bit in range(2, devices.bit_length() - 1)]

    def swap(array, mask):
        return lax.ppermute(array, "pts", [(index, index ^ mask) for index in range(devices)])

    tri_inverse = in_hbm(tri_inverse)
    me = lax.axis_index("pts").astype(jnp.int32).reshape(1)
    bias_column = jnp.broadcast_to(bias[:, None], (classes, 128))

    block = points.shape[0]
    coeffs = beta.T
    crossed = swap(coeffs[None], outer[-1])
    points, *centre_halves, coeffs = prepare(points, labels, centres, coeffs)
    centres_2 = [swap(centre_halves[0], 2)]
    far = [0]
    for mask in reversed(outer):
        coeffs = jnp.concatenate([coeffs, crossed if mask == outer[-1] else swap(coeffs, mask)])
        far = far + [offset ^ mask for offset in far]
        if mask != outer[0]:
            points, coeffs = lax.optimization_barrier((points, coeffs))
            points = jnp.concatenate([points, swap(points, mask)])
    count = len(far)
    later, coeffs = lax.optimization_barrier((centre_halves[1], coeffs))
    coeffs_2 = swap(coeffs, 2)
    centres_2.append(swap(later, 2))
    near_2 = [offset ^ 2 for offset in far]
    near_13 = [offset ^ 1 for offset in far + near_2]
    alpha, tri_02 = alpha_sum(me, tri_inverse, (far + near_2, coeffs), None, None, coeffs)
    coeffs_2, alpha, centres_2[0] = lax.optimization_barrier((coeffs_2, alpha, centres_2[0]))
    coeffs_13 = swap(jnp.concatenate([coeffs, coeffs_2]), 1)
    alpha, tri_13 = alpha_sum(me, tri_inverse, (near_13, coeffs_13), (tri_02, count, coeffs_2), alpha, points)
    points = [points, swap(points, outer[0])]

    alpha_2 = swap(alpha, 2)
    near_centres = [[centres], [swap(centres, 1)]]
    tile_00 = kernel_tile(block, points[0], near_centres, alpha)
    alpha_1 = swap(alpha, 1)
    *centres_2, alpha = lax.optimization_barrier((*centres_2, alpha))
    far_centres = [centres_2, [swap(piece, 1) for piece in centres_2]]
    tile_01 = kernel_tile(block, points[0], far_centres, tile_00)
    alpha_2, tile_01, points[1] = lax.optimization_barrier((alpha_2, tile_01, points[1]))
    alpha_3 = swap(alpha_2, 1)
    tile_10 = kernel_tile(block, points[1], near_centres, tile_01)
    tile_11 = kernel_tile(block, points[1], far_centres, tile_10)
    tiles = [[tile_00, tile_01], [tile_10, tile_11]]
    logit_sum = partial_logits(tiles, (alpha, alpha_1, alpha_2, alpha_3))

    rounded = logit_sum.astype(BF16)
    partners = sorted(far[1:], reverse=True)
    received = [swap(rounded, offset) for offset in partners]
    orders = [[far.index(held ^ offset) for held in far] for offset in partners]
    compute = residual(logit_sum, received, orders, bias_column, points)
    send, logits, resid = kernel_gradient(1, None, tiles, (compute, (logit_sum, received, bias_column, points)))
    received = swap(send, 1)
    (keep,) = kernel_gradient(0, resid, tiles)

    received_2 = swap(keep[1] + received[1], 2)
    grad = ((keep[0] + received[0] + received_2) * (1.0 / math.sqrt(total_points))).astype(BF16)

    term_3 = gradient_terms(grad, tri_13, count, count, grad)
    received_3 = swap(term_3, 1)
    term_1 = gradient_terms(grad, tri_13, 0, count, term_3)
    received_1 = swap(term_1, 1)
    term_2 = gradient_terms(grad, tri_02, count, count, term_1)
    ahead = (term_2 + received_3).astype(BF16)
    received_2 = swap(ahead, 2)
    term_0 = gradient_terms(grad, tri_02, 0, count, ahead)
    total = term_0 + received_1 + received_2.astype(F32)
    gradient = total[0]
    for offset in sorted(far[1:], reverse=True):
        gradient = gradient + swap(total[far.index(offset)].astype(BF16), offset).astype(F32)
    return (gradient.T, logits.T)


def solution(mesh):
    return jax.shard_map(
        on_device,
        mesh=mesh,
        in_specs=(
            P(("groups", "pts"), None),
            P(("groups", "pts")),
            P(("groups", "pts"), None),
            P(("groups", "pts"), None),
            P(("groups", "pts"), None),
            P("groups"),
        ),
        out_specs=(P(("groups", "pts"), None), P(("groups", "pts"), None)),
        check_vma=False,
    )
```

```python
import math

import jax
import jax.numpy as jnp
from jax import lax
from jax.experimental import pallas as pl
from jax.experimental.pallas import tpu as pltpu
from jax.sharding import PartitionSpec as P

BF16 = jnp.bfloat16
F32 = jnp.float32
ROWS_BY_ROWS = (((1,), (1,)), ((), ()))
MIB = 1 << 20
IN_FLIGHT = 3


def params(mib):
    return pltpu.CompilerParams(vmem_limit_bytes=mib * MIB)


def in_hbm(array):
    return pltpu.with_memory_space_constraint(array, pltpu.HBM)


def in_vmem():
    return pl.BlockSpec(memory_space=pltpu.VMEM)


def anywhere():
    return pl.BlockSpec(memory_space=pl.ANY)


def in_smem():
    return pl.BlockSpec(memory_space=pltpu.SMEM)


def cost(flops, bytes_accessed):
    return pl.CostEstimate(flops=int(flops), bytes_accessed=int(bytes_accessed), transcendentals=0)


def alpha_sum(me, tri, brought, known, total, after):
    offsets, betas = brought
    rows = tri.shape[0]
    classes, width = betas.shape[1:]
    count = len(offsets)
    ahead = min(IN_FLIGHT, count)
    last = total is not None

    def body(me_ref, tri_ref, after_ref, beta_ref, *refs):
        known_refs, (out_ref, held_ref, sems) = refs[:-3], refs[-3:]
        copies = [
            pltpu.make_async_copy(
                tri_ref.at[:, pl.ds(pl.multiple_of((me_ref[0] ^ offset) * width, width), width)],
                held_ref.at[at],
                sems.at[at],
            )
            for at, offset in enumerate(offsets)
        ]
        for copy in copies[:ahead]:
            copy.start()
        acc = None
        if last:
            total_ref, block_ref, known_beta_ref = known_refs
            acc = total_ref[...]
            for at in range(known_beta_ref.shape[0]):
                acc = acc + lax.dot_general(
                    known_beta_ref[at], block_ref[known[1] + at], ROWS_BY_ROWS, preferred_element_type=F32
                )
        for at in range(count):
            copies[at].wait()
            if at + ahead < count:
                copies[at + ahead].start()
            if at < betas.shape[0]:
                term = lax.dot_general(beta_ref[at], held_ref[at], ROWS_BY_ROWS, preferred_element_type=F32)
                acc = term if acc is None else acc + term
        out_ref[...] = acc.astype(out_ref.dtype)

    operands = (me, tri, after, betas)
    if last:
        operands += (total, pltpu.with_memory_space_constraint(known[0], pltpu.VMEM), known[2])
    return pl.pallas_call(
        body,
        out_shape=[
            jax.ShapeDtypeStruct((classes, rows), BF16 if last else F32),
            pltpu.VMEM((count, rows, width), BF16),
        ],
        in_specs=[in_smem(), anywhere(), anywhere()] + [in_vmem()] * (len(operands) - 3),
        out_specs=[in_vmem(), in_vmem()],
        scratch_shapes=[pltpu.SemaphoreType.DMA((count,))],
        compiler_params=params(8),
        cost_estimate=cost(2 * rows * count * width * 128, 2 * rows * count * width),
        name="alpha_sum",
    )(*operands)


def prepare(points, labels, centres, beta):
    half = centres.shape[0] // 2
    block, features = points.shape
    classes = beta.shape[0]

    def body(points_ref, labels_ref, centres_ref, beta_ref, ext_ref, first_ref, second_ref, held_ref, row_ref, sems):
        moves = (
            (labels_ref, row_ref),
            (centres_ref.at[pl.ds(0, half)], first_ref),
            (points_ref, ext_ref.at[0, pl.ds(0, block)]),
            (beta_ref, held_ref.at[0]),
            (centres_ref.at[pl.ds(half, half)], second_ref),
        )
        copies = [pltpu.make_async_copy(source, target, sems.at[at]) for at, (source, target) in enumerate(moves)]
        for copy in copies:
            copy.start()
        class_column = lax.broadcasted_iota(jnp.int32, (classes, block), 0)
        ext_ref[0, block:, :] = jnp.zeros((classes, features), BF16)
        copies[0].wait()
        ext_ref[0, block:, :block] = jnp.where(row_ref[...] == class_column, 1.0, 0.0).astype(BF16)
        for copy in copies[1:]:
            copy.wait()

    return pl.pallas_call(
        body,
        out_shape=[
            pltpu.VMEM((1, block + classes, features), BF16),
            pltpu.VMEM((half, features), BF16),
            pltpu.VMEM((half, features), BF16),
            pltpu.VMEM((1, *beta.shape), BF16),
        ],
        in_specs=[anywhere()] * 4,
        out_specs=[in_vmem()] * 4,
        scratch_shapes=[pltpu.VMEM((1, block), jnp.int32), pltpu.SemaphoreType.DMA((5,))],
        compiler_params=params(8),
        cost_estimate=cost(1024, 4 * centres.size),
        name="prepare",
    )(in_hbm(points), in_hbm(labels[None, :]), in_hbm(centres), in_hbm(beta))


def gradient_terms(grad, blocks, first, count, after):
    classes, rows = grad.shape
    width = blocks.shape[2]

    def body(after_ref, grad_ref, block_ref, out_ref):
        for at in range(count):
            out_ref[at] = jnp.dot(grad_ref[...], block_ref[first + at], preferred_element_type=F32)

    return pl.pallas_call(
        body,
        out_shape=jax.ShapeDtypeStruct((count, classes, width), F32),
        in_specs=[anywhere(), in_vmem(), in_vmem()],
        out_specs=in_vmem(),
        compiler_params=params(8),
        cost_estimate=cost(2 * rows * count * width * 128, 1024),
        name="gradient_terms",
    )(after, grad, pltpu.with_memory_space_constraint(blocks, pltpu.VMEM))


def kernel_tile(block, points, centre_blocks, after):
    count, _, features = points.shape
    local = sum(piece.shape[0] for piece in centre_blocks[0])
    factor = 1.0 / math.sqrt(features)
    pieces = [piece for pieces in centre_blocks for piece in pieces]
    total = count * block

    def body(point_ref, *refs):
        piece_refs, out_ref = refs[:-2], refs[-1]
        row = 0
        for piece_ref in piece_refs:
            which, first, rows = row // local, row % local, piece_ref.shape[0]
            for at in range(count):
                inner = lax.dot_general(
                    piece_ref[...], point_ref[at, :block], ROWS_BY_ROWS, preferred_element_type=F32
                )
                value = inner * factor + 1.0
                out_ref[which, first : first + rows, at * block : (at + 1) * block] = (
                    value * value * value
                ).astype(BF16)
            row += rows

    return pl.pallas_call(
        body,
        out_shape=pltpu.VMEM((len(centre_blocks), local, total), BF16),
        in_specs=[in_vmem()] * (1 + len(pieces)) + [anywhere()],
        out_specs=in_vmem(),
        compiler_params=params(8),
        cost_estimate=cost(1024, 1024),
        name="kernel_tile",
    )(points, *pieces, after)


def place_of(row, index):
    for which, tile in enumerate(row):
        if index < tile.shape[0]:
            return which, index
        index -= tile.shape[0]


def partial_logits(tiles, alphas):
    classes = alphas[0].shape[0]
    sizes = [row[0].shape[2] for row in tiles]
    flat = [tile for row in tiles for tile in row]

    def body(*refs):
        alpha_refs, tile_refs, out_ref = refs[: len(alphas)], refs[len(alphas) : -1], refs[-1]
        for part, size in enumerate(sizes):
            first = sum(sizes[:part])
            held = sum(len(row) for row in tiles[:part])
            acc = None
            for index in range(len(alphas)):
                which, at = place_of(tiles[part], index)
                term = jnp.dot(alpha_refs[index][...], tile_refs[held + which][at], preferred_element_type=F32)
                acc = term if acc is None else acc + term
            out_ref[:, first : first + size] = acc

    return pl.pallas_call(
        body,
        out_shape=jax.ShapeDtypeStruct((classes, sum(sizes)), F32),
        in_specs=[in_vmem()] * (len(alphas) + len(flat)),
        out_specs=in_vmem(),
        compiler_params=params(8),
        cost_estimate=cost(2 * sum(tile.size for tile in flat) * 128, 1024),
        name="partial_logits",
    )(*alphas, *flat)


def residual(logit_sum, received, orders, bias, points):
    classes, total = logit_sum.shape
    block = total // len(orders[0])
    blocks = [(which, at) for which, array in enumerate(points) for at in range(array.shape[0])]

    def compute(sum_ref, bias_ref, received_refs, point_refs, logits_ref, resid_ref):
        for at in range(len(blocks)):
            here = slice(at * block, (at + 1) * block)
            logits = sum_ref[:, here]
            for received_ref, order in zip(received_refs, orders):
                there = slice(order[at] * block, (order[at] + 1) * block)
                logits = logits + received_ref[:, there].astype(F32)
            logits = logits + bias_ref[:, :1]
            if at == 0:
                logits_ref[...] = logits
            which, row = blocks[at]
            onehot = point_refs[which][row, block : block + classes, :block].astype(F32)
            resid_ref[:, here] = (jax.nn.sigmoid(logits) - onehot).astype(BF16)

    return compute


def kernel_gradient(parity, resid, tiles, residual_of=None):
    flat = [tile for row in tiles for tile in row]
    n_parts = len(tiles[0])
    local = flat[0].shape[1]
    sizes = [row[0].shape[2] for row in tiles]
    total = sum(sizes)
    out_shape = []
    if residual_of is None:
        operands = [resid]
    else:
        compute, (logit_sum, received, bias, points) = residual_of
        operands = [logit_sum, bias, *received, *points]
        n_first = 2 + len(received)
        block = points[0].shape[1] - logit_sum.shape[0]
        out_shape = [jax.ShapeDtypeStruct((logit_sum.shape[0], block), F32)]
        out_shape.append(jax.ShapeDtypeStruct(logit_sum.shape, BF16))
    classes = operands[0].shape[0]
    n_operands = len(operands)

    def body(*refs):
        tile_refs = refs[n_operands : n_operands + len(flat)]
        out_ref, *more_refs = refs[n_operands + len(flat) :]
        resid_ref = refs[0]
        if residual_of is not None:
            logits_ref, resid_ref = more_refs
            compute(*refs[:2], refs[2:n_first], refs[n_first:n_operands], logits_ref, resid_ref)
        for which in range(n_parts):
            acc = None
            for part, size in enumerate(sizes):
                first = sum(sizes[:part])
                held = sum(len(row) for row in tiles[:part])
                array, at = place_of(tiles[part], 2 * which + parity)
                term = lax.dot_general(
                    resid_ref[:, first : first + size],
                    tile_refs[held + array][at],
                    ROWS_BY_ROWS,
                    preferred_element_type=F32,
                )
                acc = term if acc is None else acc + term
            out_ref[which] = acc

    return pl.pallas_call(
        body,
        out_shape=[jax.ShapeDtypeStruct((n_parts, classes, local), F32)] + out_shape,
        in_specs=[in_vmem()] * (n_operands + len(flat)),
        out_specs=[in_vmem()] * (1 + len(out_shape)),
        compiler_params=params(8),
        cost_estimate=cost(2 * total * n_parts * local * 128, 1024),
        name="kernel_gradient",
    )(*operands, *flat)


def on_device(points, labels, centres, tri_inverse, beta, bias):
    devices = lax.axis_size("pts")
    local_centres, classes = beta.shape
    total_points = points.shape[0] * devices
    outer = [1 << bit for bit in range(2, devices.bit_length() - 1)]

    def swap(array, mask):
        return lax.ppermute(array, "pts", [(index, index ^ mask) for index in range(devices)])

    tri_inverse = in_hbm(tri_inverse)
    me = lax.axis_index("pts").astype(jnp.int32).reshape(1)
    bias_column = jnp.broadcast_to(bias[:, None], (classes, 128))

    block = points.shape[0]
    coeffs = beta.T
    crossed = swap(coeffs[None], outer[-1])
    points, *centre_halves, coeffs = prepare(points, labels, centres, coeffs)
    centres_2 = [swap(centre_halves[0], 2)]
    far = [0]
    for mask in reversed(outer):
        coeffs = jnp.concatenate([coeffs, crossed if mask == outer[-1] else swap(coeffs, mask)])
        far = far + [offset ^ mask for offset in far]
        if mask != outer[0]:
            points, coeffs = lax.optimization_barrier((points, coeffs))
            points = jnp.concatenate([points, swap(points, mask)])
    count = len(far)
    later, coeffs = lax.optimization_barrier((centre_halves[1], coeffs))
    coeffs_2 = swap(coeffs, 2)
    centres_2.append(swap(later, 2))
    near_2 = [offset ^ 2 for offset in far]
    near_13 = [offset ^ 1 for offset in far + near_2]
    alpha, tri_02 = alpha_sum(me, tri_inverse, (far + near_2, coeffs), None, None, coeffs)
    coeffs_2, alpha, centres_2[0] = lax.optimization_barrier((coeffs_2, alpha, centres_2[0]))
    coeffs_13 = swap(jnp.concatenate([coeffs, coeffs_2]), 1)
    alpha, tri_13 = alpha_sum(me, tri_inverse, (near_13, coeffs_13), (tri_02, count, coeffs_2), alpha, points)
    points = [points, swap(points, outer[0])]

    alpha_2 = swap(alpha, 2)
    near_centres = [[centres], [swap(centres, 1)]]
    tile_00 = kernel_tile(block, points[0], near_centres, alpha)
    alpha_1 = swap(alpha, 1)
    *centres_2, alpha = lax.optimization_barrier((*centres_2, alpha))
    far_centres = [centres_2, [swap(piece, 1) for piece in centres_2]]
    tile_01 = kernel_tile(block, points[0], far_centres, tile_00)
    alpha_2, tile_01, points[1] = lax.optimization_barrier((alpha_2, tile_01, points[1]))
    alpha_3 = swap(alpha_2, 1)
    tile_1 = kernel_tile(block, points[1], near_centres + far_centres, tile_01)
    tiles = [[tile_00, tile_01], [tile_1]]
    logit_sum = partial_logits(tiles, (alpha, alpha_1, alpha_2, alpha_3))

    rounded = logit_sum.astype(BF16)
    partners = sorted(far[1:], reverse=True)
    received = [swap(rounded, offset) for offset in partners]
    orders = [[far.index(held ^ offset) for held in far] for offset in partners]
    compute = residual(logit_sum, received, orders, bias_column, points)
    send, logits, resid = kernel_gradient(1, None, tiles, (compute, (logit_sum, received, bias_column, points)))
    received = swap(send, 1)
    (keep,) = kernel_gradient(0, resid, tiles)

    received_2 = swap(keep[1] + received[1], 2)
    grad = ((keep[0] + received[0] + received_2) * (1.0 / math.sqrt(total_points))).astype(BF16)

    term_3 = gradient_terms(grad, tri_13, count, count, grad)
    received_3 = swap(term_3, 1)
    term_1 = gradient_terms(grad, tri_13, 0, count, term_3)
    received_1 = swap(term_1, 1)
    term_2 = gradient_terms(grad, tri_02, count, count, term_1)
    ahead = (term_2 + received_3).astype(BF16)
    received_2 = swap(ahead, 2)
    term_0 = gradient_terms(grad, tri_02, 0, count, ahead)
    total = term_0 + received_1 + received_2.astype(F32)
    gradient = total[0]
    for offset in sorted(far[1:], reverse=True):
        gradient = gradient + swap(total[far.index(offset)].astype(BF16), offset).astype(F32)
    return (gradient.T, logits.T)


def solution(mesh):
    return jax.shard_map(
        on_device,
        mesh=mesh,
        in_specs=(
            P(("groups", "pts"), None),
            P(("groups", "pts")),
            P(("groups", "pts"), None),
            P(("groups", "pts"), None),
            P(("groups", "pts"), None),
            P("groups"),
        ),
        out_specs=(P(("groups", "pts"), None), P(("groups", "pts"), None)),
        check_vma=False,
    )
```

```python
import math

import jax
import jax.numpy as jnp
from jax import lax
from jax.experimental import pallas as pl
from jax.experimental.pallas import tpu as pltpu
from jax.sharding import PartitionSpec as P

BF16 = jnp.bfloat16
F32 = jnp.float32
ROWS_BY_ROWS = (((1,), (1,)), ((), ()))
MIB = 1 << 20
IN_FLIGHT = 4


def params(mib):
    return pltpu.CompilerParams(vmem_limit_bytes=mib * MIB)


def in_hbm(array):
    return pltpu.with_memory_space_constraint(array, pltpu.HBM)


def in_vmem():
    return pl.BlockSpec(memory_space=pltpu.VMEM)


def anywhere():
    return pl.BlockSpec(memory_space=pl.ANY)


def in_smem():
    return pl.BlockSpec(memory_space=pltpu.SMEM)


def cost(flops, bytes_accessed):
    return pl.CostEstimate(flops=int(flops), bytes_accessed=int(bytes_accessed), transcendentals=0)


def alpha_sum(me, tri, brought, known, total, after):
    offsets, betas = brought
    rows = tri.shape[0]
    classes, width = betas.shape[1:]
    count = len(offsets)
    ahead = min(IN_FLIGHT, count)
    last = total is not None

    def body(me_ref, tri_ref, after_ref, beta_ref, *refs):
        known_refs, (out_ref, held_ref, sems) = refs[:-3], refs[-3:]
        copies = [
            pltpu.make_async_copy(
                tri_ref.at[:, pl.ds(pl.multiple_of((me_ref[0] ^ offset) * width, width), width)],
                held_ref.at[at],
                sems.at[at],
            )
            for at, offset in enumerate(offsets)
        ]
        for copy in copies[:ahead]:
            copy.start()
        acc = None
        if last:
            total_ref, block_ref, known_beta_ref = known_refs
            acc = total_ref[...]
            for at in range(known_beta_ref.shape[0]):
                acc = acc + lax.dot_general(
                    known_beta_ref[at], block_ref[known[1] + at], ROWS_BY_ROWS, preferred_element_type=F32
                )
        for at in range(count):
            copies[at].wait()
            if at + ahead < count:
                copies[at + ahead].start()
            if at < betas.shape[0]:
                term = lax.dot_general(beta_ref[at], held_ref[at], ROWS_BY_ROWS, preferred_element_type=F32)
                acc = term if acc is None else acc + term
        out_ref[...] = acc.astype(out_ref.dtype)

    operands = (me, tri, after, betas)
    if last:
        operands += (total, pltpu.with_memory_space_constraint(known[0], pltpu.VMEM), known[2])
    return pl.pallas_call(
        body,
        out_shape=[
            jax.ShapeDtypeStruct((classes, rows), BF16 if last else F32),
            pltpu.VMEM((count, rows, width), BF16),
        ],
        in_specs=[in_smem(), anywhere(), anywhere()] + [in_vmem()] * (len(operands) - 3),
        out_specs=[in_vmem(), in_vmem()],
        scratch_shapes=[pltpu.SemaphoreType.DMA((count,))],
        compiler_params=params(8),
        cost_estimate=cost(2 * rows * count * width * 128, 2 * rows * count * width),
        name="alpha_sum",
    )(*operands)


def prepare(points, labels, centres, beta):
    half = centres.shape[0] // 2
    block, features = points.shape
    classes = beta.shape[0]

    def body(points_ref, labels_ref, centres_ref, beta_ref, ext_ref, first_ref, second_ref, held_ref, row_ref, sems):
        moves = (
            (labels_ref, row_ref),
            (centres_ref.at[pl.ds(0, half)], first_ref),
            (points_ref, ext_ref.at[0, pl.ds(0, block)]),
            (beta_ref, held_ref.at[0]),
            (centres_ref.at[pl.ds(half, half)], second_ref),
        )
        copies = [pltpu.make_async_copy(source, target, sems.at[at]) for at, (source, target) in enumerate(moves)]
        for copy in copies:
            copy.start()
        class_column = lax.broadcasted_iota(jnp.int32, (classes, block), 0)
        ext_ref[0, block:, :] = jnp.zeros((classes, features), BF16)
        copies[0].wait()
        ext_ref[0, block:, :block] = jnp.where(row_ref[...] == class_column, 1.0, 0.0).astype(BF16)
        for copy in copies[1:]:
            copy.wait()

    return pl.pallas_call(
        body,
        out_shape=[
            pltpu.VMEM((1, block + classes, features), BF16),
            pltpu.VMEM((half, features), BF16),
            pltpu.VMEM((half, features), BF16),
            pltpu.VMEM((1, *beta.shape), BF16),
        ],
        in_specs=[anywhere()] * 4,
        out_specs=[in_vmem()] * 4,
        scratch_shapes=[pltpu.VMEM((1, block), jnp.int32), pltpu.SemaphoreType.DMA((5,))],
        compiler_params=params(8),
        cost_estimate=cost(1024, 4 * centres.size),
        name="prepare",
    )(in_hbm(points), in_hbm(labels[None, :]), in_hbm(centres), in_hbm(beta))


def gradient_terms(grad, blocks, first, count, after):
    classes, rows = grad.shape
    width = blocks.shape[2]

    def body(after_ref, grad_ref, block_ref, out_ref):
        for at in range(count):
            out_ref[at] = jnp.dot(grad_ref[...], block_ref[first + at], preferred_element_type=F32)

    return pl.pallas_call(
        body,
        out_shape=jax.ShapeDtypeStruct((count, classes, width), F32),
        in_specs=[anywhere(), in_vmem(), in_vmem()],
        out_specs=in_vmem(),
        compiler_params=params(8),
        cost_estimate=cost(2 * rows * count * width * 128, 1024),
        name="gradient_terms",
    )(after, grad, pltpu.with_memory_space_constraint(blocks, pltpu.VMEM))


def kernel_tile(block, points, centre_blocks, after):
    count, _, features = points.shape
    local = sum(piece.shape[0] for piece in centre_blocks[0])
    factor = 1.0 / math.sqrt(features)
    pieces = [piece for pieces in centre_blocks for piece in pieces]
    total = count * block

    def body(point_ref, *refs):
        piece_refs, out_ref = refs[:-2], refs[-1]
        row = 0
        for piece_ref in piece_refs:
            which, first, rows = row // local, row % local, piece_ref.shape[0]
            for at in range(count):
                inner = lax.dot_general(
                    piece_ref[...], point_ref[at, :block], ROWS_BY_ROWS, preferred_element_type=F32
                )
                value = inner * factor + 1.0
                out_ref[which, first : first + rows, at * block : (at + 1) * block] = (
                    value * value * value
                ).astype(BF16)
            row += rows

    return pl.pallas_call(
        body,
        out_shape=pltpu.VMEM((len(centre_blocks), local, total), BF16),
        in_specs=[in_vmem()] * (1 + len(pieces)) + [anywhere()],
        out_specs=in_vmem(),
        compiler_params=params(8),
        cost_estimate=cost(1024, 1024),
        name="kernel_tile",
    )(points, *pieces, after)


def place_of(row, index):
    for which, tile in enumerate(row):
        if index < tile.shape[0]:
            return which, index
        index -= tile.shape[0]


def partial_logits(tiles, alphas):
    classes = alphas[0].shape[0]
    sizes = [row[0].shape[2] for row in tiles]
    flat = [tile for row in tiles for tile in row]

    def body(*refs):
        alpha_refs, tile_refs, out_ref = refs[: len(alphas)], refs[len(alphas) : -1], refs[-1]
        for part, size in enumerate(sizes):
            first = sum(sizes[:part])
            held = sum(len(row) for row in tiles[:part])
            acc = None
            for index in range(len(alphas)):
                which, at = place_of(tiles[part], index)
                term = jnp.dot(alpha_refs[index][...], tile_refs[held + which][at], preferred_element_type=F32)
                acc = term if acc is None else acc + term
            out_ref[:, first : first + size] = acc

    return pl.pallas_call(
        body,
        out_shape=jax.ShapeDtypeStruct((classes, sum(sizes)), F32),
        in_specs=[in_vmem()] * (len(alphas) + len(flat)),
        out_specs=in_vmem(),
        compiler_params=params(8),
        cost_estimate=cost(2 * sum(tile.size for tile in flat) * 128, 1024),
        name="partial_logits",
    )(*alphas, *flat)


def residual(logit_sum, received, orders, bias, points):
    classes, total = logit_sum.shape
    block = total // len(orders[0])
    blocks = [(which, at) for which, array in enumerate(points) for at in range(array.shape[0])]

    def compute(sum_ref, bias_ref, received_refs, point_refs, logits_ref, resid_ref):
        for at in range(len(blocks)):
            here = slice(at * block, (at + 1) * block)
            logits = sum_ref[:, here]
            for received_ref, order in zip(received_refs, orders):
                there = slice(order[at] * block, (order[at] + 1) * block)
                logits = logits + received_ref[:, there].astype(F32)
            logits = logits + bias_ref[:, :1]
            if at == 0:
                logits_ref[...] = logits
            which, row = blocks[at]
            onehot = point_refs[which][row, block : block + classes, :block].astype(F32)
            resid_ref[:, here] = (jax.nn.sigmoid(logits) - onehot).astype(BF16)

    return compute


def kernel_gradient(parity, resid, tiles, residual_of=None):
    flat = [tile for row in tiles for tile in row]
    n_parts = len(tiles[0])
    local = flat[0].shape[1]
    sizes = [row[0].shape[2] for row in tiles]
    total = sum(sizes)
    out_shape = []
    if residual_of is None:
        operands = [resid]
    else:
        compute, (logit_sum, received, bias, points) = residual_of
        operands = [logit_sum, bias, *received, *points]
        n_first = 2 + len(received)
        block = points[0].shape[1] - logit_sum.shape[0]
        out_shape = [jax.ShapeDtypeStruct((logit_sum.shape[0], block), F32)]
        out_shape.append(jax.ShapeDtypeStruct(logit_sum.shape, BF16))
    classes = operands[0].shape[0]
    n_operands = len(operands)

    def body(*refs):
        tile_refs = refs[n_operands : n_operands + len(flat)]
        out_ref, *more_refs = refs[n_operands + len(flat) :]
        resid_ref = refs[0]
        if residual_of is not None:
            logits_ref, resid_ref = more_refs
            compute(*refs[:2], refs[2:n_first], refs[n_first:n_operands], logits_ref, resid_ref)
        for which in range(n_parts):
            acc = None
            for part, size in enumerate(sizes):
                first = sum(sizes[:part])
                held = sum(len(row) for row in tiles[:part])
                array, at = place_of(tiles[part], 2 * which + parity)
                term = lax.dot_general(
                    resid_ref[:, first : first + size],
                    tile_refs[held + array][at],
                    ROWS_BY_ROWS,
                    preferred_element_type=F32,
                )
                acc = term if acc is None else acc + term
            out_ref[which] = acc

    return pl.pallas_call(
        body,
        out_shape=[jax.ShapeDtypeStruct((n_parts, classes, local), F32)] + out_shape,
        in_specs=[in_vmem()] * (n_operands + len(flat)),
        out_specs=[in_vmem()] * (1 + len(out_shape)),
        compiler_params=params(8),
        cost_estimate=cost(2 * total * n_parts * local * 128, 1024),
        name="kernel_gradient",
    )(*operands, *flat)


def on_device(points, labels, centres, tri_inverse, beta, bias):
    devices = lax.axis_size("pts")
    local_centres, classes = beta.shape
    total_points = points.shape[0] * devices
    outer = [1 << bit for bit in range(2, devices.bit_length() - 1)]

    def swap(array, mask):
        return lax.ppermute(array, "pts", [(index, index ^ mask) for index in range(devices)])

    tri_inverse = in_hbm(tri_inverse)
    me = lax.axis_index("pts").astype(jnp.int32).reshape(1)
    bias_column = jnp.broadcast_to(bias[:, None], (classes, 128))

    block = points.shape[0]
    coeffs = beta.T
    crossed = swap(coeffs[None], outer[-1])
    points, *centre_halves, coeffs = prepare(points, labels, centres, coeffs)
    centres_2 = [swap(centre_halves[0], 2)]
    far = [0]
    for mask in reversed(outer):
        coeffs = jnp.concatenate([coeffs, crossed if mask == outer[-1] else swap(coeffs, mask)])
        far = far + [offset ^ mask for offset in far]
        if mask != outer[0]:
            points, coeffs = lax.optimization_barrier((points, coeffs))
            points = jnp.concatenate([points, swap(points, mask)])
    count = len(far)
    later, coeffs = lax.optimization_barrier((centre_halves[1], coeffs))
    coeffs_2 = swap(coeffs, 2)
    centres_2.append(swap(later, 2))
    near_2 = [offset ^ 2 for offset in far]
    near_13 = [offset ^ 1 for offset in far + near_2]
    alpha, tri_02 = alpha_sum(me, tri_inverse, (far + near_2, coeffs), None, None, coeffs)
    coeffs_2, alpha, centres_2[0] = lax.optimization_barrier((coeffs_2, alpha, centres_2[0]))
    coeffs_13 = swap(jnp.concatenate([coeffs, coeffs_2]), 1)
    alpha, tri_13 = alpha_sum(me, tri_inverse, (near_13, coeffs_13), (tri_02, count, coeffs_2), alpha, points)
    points = [points, swap(points, outer[0])]

    alpha_2 = swap(alpha, 2)
    near_centres = [[centres], [swap(centres, 1)]]
    tile_00 = kernel_tile(block, points[0], near_centres, alpha)
    alpha_1 = swap(alpha, 1)
    *centres_2, alpha = lax.optimization_barrier((*centres_2, alpha))
    far_centres = [centres_2, [swap(piece, 1) for piece in centres_2]]
    tile_01 = kernel_tile(block, points[0], far_centres, tile_00)
    alpha_2, tile_01, points[1] = lax.optimization_barrier((alpha_2, tile_01, points[1]))
    alpha_3 = swap(alpha_2, 1)
    tile_1 = kernel_tile(block, points[1], near_centres + far_centres, tile_01)
    tiles = [[tile_00, tile_01], [tile_1]]
    logit_sum = partial_logits(tiles, (alpha, alpha_1, alpha_2, alpha_3))

    rounded = logit_sum.astype(BF16)
    partners = sorted(far[1:], reverse=True)
    received = [swap(rounded, offset) for offset in partners]
    orders = [[far.index(held ^ offset) for held in far] for offset in partners]
    compute = residual(logit_sum, received, orders, bias_column, points)
    send, logits, resid = kernel_gradient(1, None, tiles, (compute, (logit_sum, received, bias_column, points)))
    received = swap(send, 1)
    (keep,) = kernel_gradient(0, resid, tiles)

    received_2 = swap(keep[1] + received[1], 2)
    grad = ((keep[0] + received[0] + received_2) * (1.0 / math.sqrt(total_points))).astype(BF16)

    term_3 = gradient_terms(grad, tri_13, count, count, grad)
    received_3 = swap(term_3, 1)
    term_1 = gradient_terms(grad, tri_13, 0, count, term_3)
    received_1 = swap(term_1, 1)
    term_2 = gradient_terms(grad, tri_02, count, count, term_1)
    ahead = (term_2 + received_3).astype(BF16)
    received_2 = swap(ahead, 2)
    term_0 = gradient_terms(grad, tri_02, 0, count, ahead)
    total = term_0 + received_1 + received_2.astype(F32)
    gradient = total[0]
    for offset in sorted(far[1:], reverse=True):
        gradient = gradient + swap(total[far.index(offset)].astype(BF16), offset).astype(F32)
    return (gradient.T, logits.T)


def solution(mesh):
    return jax.shard_map(
        on_device,
        mesh=mesh,
        in_specs=(
            P(("groups", "pts"), None),
            P(("groups", "pts")),
            P(("groups", "pts"), None),
            P(("groups", "pts"), None),
            P(("groups", "pts"), None),
            P("groups"),
        ),
        out_specs=(P(("groups", "pts"), None), P(("groups", "pts"), None)),
        check_vma=False,
    )
```
